32 devices in a mesh: dp: 16 (over z, x, core), mp: 2 (over y).
Axes of the slice: x: 2, y: 2, z: 4, core: 2. Of those that a mesh axis runs over, the one named last changes fastest.
Arguments:
- segment_matrix: float32 [8192, 32], P('dp'), may hold values from -30 to 30
- filled_sequence_segments: int32 [16, 64], P('dp'), may hold values from 1 to 64, 512 in all within a row
- leading_filler_number: int32 [16, 64], P('dp'), may hold values from 0 to 3
- segment_lifting_matrix: bfloat16 [32, 1280], P(None, 'dp'), may hold values from -1 to 1
- triple_projector_matrix: bfloat16 [2, 3, 1280, 1280], P(None, None, 'dp', 'mp'), may hold values from -0.15625 to 0.15625
- mixer_exit_matrix: bfloat16 [2, 1280, 1280], P(None, 'mp', 'dp'), may hold values from -0.3125 to 0.3125
- widen_matrix: bfloat16 [2, 1280, 1280], P(None, 'dp', 'mp'), may hold values from -0.15625 to 0.15625
- shrink_matrix: bfloat16 [2, 1280, 1280], P(None, 'mp', 'dp'), may hold values from -0.25 to 0.25
- normalizer_factors: bfloat16 [2, 2, 1280], P(None, None, 'dp'), may hold values from 0.099609375 to 1.8984375
- prediction_matrix: bfloat16 [1280, 1280], P('dp', 'mp'), may hold values from -0.15625 to 0.15625
- prediction_sensitivity: bfloat16 [8192, 1280], P('dp', 'mp'), may hold values from -6 to 6
Outputs:
- predictions: float32 [8192, 1280], P('dp', 'mp')
- patches_grad: float32 [8192, 32], P('dp')
- w_in_grad: float32 [32, 1280], P(None, 'dp')
- w_qkv_grad: float32 [2, 3, 1280, 1280], P(None, None, 'dp', 'mp')
- w_attn_grad: float32 [2, 1280, 1280], P(None, 'mp', 'dp')
- w_up_grad: float32 [2, 1280, 1280], P(None, 'dp', 'mp')
- w_down_grad: float32 [2, 1280, 1280], P(None, 'mp', 'dp')
- gains_grad: float32 [2, 2, 1280], P(None, None, 'dp')
- w_head_grad: float32 [1280, 1280], P('dp', 'mp')
The draws below stay inside these ranges and needn't reach their ends.
Inputs may be any that keep to these rules, and one draw needn't show every extreme that they name: `filled_sequence_segments`: each row sums to 512, and has an entry equal to 64.
All inputs are finite; a program needn't handle non-finite values.
Results may differ from the reference program's by a relative error of at most 0.033.
Values may be sent and summed in bfloat16 or wider, within the bound.
No kernel may reach another device: no remote copies, remote signals or barrier semaphores. Data moves between devices by JAX's collectives and lax.ppermute only.
A program may use at most 192 MiB of HBM per device.

```python
import math
import jax
import jax.numpy as jnp
import numpy as np
from jax import lax

MODEL_WIDTH = 1280
HEADS = 16
HEAD = 80
FF = 1280
PATCH = 32
HORIZON_STEPS = 1280
LAYERS = 2
TOK_DEV = 512
SER_DEV = 64
MAXP = 64
KEYS_BACK = 128
QBLOCK = 512
SEGMENT_TOTAL = 8192
N_DP = 16


def draw_segment_matrix(key, part):
    key = jax.random.fold_in(key, 11)
    noise_key, scale_key, shift_key = jax.random.split(key, 3)
    noise = jax.random.truncated_normal(noise_key, -4.0, 4.0, (SEGMENT_TOTAL, PATCH), jnp.float32)
    scale = jnp.exp(jax.random.uniform(scale_key, (SEGMENT_TOTAL, 1), jnp.float32, math.log(0.25), math.log(4.0)))
    shift = jax.random.truncated_normal(shift_key, -2.0, 2.0, (SEGMENT_TOTAL, 1), jnp.float32)
    return scale * (noise + shift)


def with_ends(result, stream_key, smallest, top_value):
    index_at = [jax.random.randint(jax.random.fold_in(stream_key, axis), (), 0, length) for axis, length in enumerate(result.shape)]
    widest = result.shape.index(max(result.shape))
    beside = index_at[:widest] + [(index_at[widest] + 1) % result.shape[widest]] + index_at[widest + 1:]
    return result.at[tuple(index_at)].set(smallest).at[tuple(beside)].set(top_value)


def block_levels(key, dims, pieces, low, top_value):
    def one(axis_at, shards_of):
        draws = jax.random.uniform(jax.random.fold_in(jax.random.fold_in(key, 6), axis_at), (shards_of,), jnp.float32, low / len(pieces), top_value / len(pieces))
        return jnp.repeat(jnp.exp(draws), dims[axis_at] // shards_of).reshape((-1,) + (1,) * (len(dims) - axis_at - 1))

    loudness = one(*pieces[0])
    for cut in pieces[1:]:
        loudness = loudness * one(*cut)
    return loudness


def split_up(count, total, bound, slope):
    weights = [(1 << 20) // math.isqrt(grade ** slope) + 1 for grade in range(2, count + 1)]
    rest, holding = total - bound - (count - 1), [1] * (count - 1)
    while rest > 0:
        movable = [i for i in range(count - 1) if holding[i] < bound]
        pool, left = sum([weights[i] for i in movable]), rest
        for i in movable:
            extra = min(bound - holding[i], max(1, left * weights[i] // pool), rest)
            holding[i] = holding[i] + extra
            rest = rest - extra
    return np.array([bound] + holding)


def ragged_sizes(rng, number_of, total, most, skew):
    if number_of == 2:
        one = jax.random.randint(rng, (), max(1, total - most), min(most, total - 1) + 1)
        return jnp.stack([one, total - one])
    tallies = jnp.asarray(split_up(number_of, total, most, skew), jnp.int32)
    twos = (number_of - 1) // 2
    source_of, receiver = tallies[1:1 + 2 * twos:2], tallies[2:2 + 2 * twos:2]
    slack = jnp.minimum(source_of - 1, most - receiver)
    shifted = jax.random.randint(jax.random.fold_in(rng, 1), (twos,), 0, 1 << 20) % (slack + 1)
    tallies = tallies.at[1:1 + 2 * twos:2].set(source_of - shifted).at[2:2 + 2 * twos:2].set(receiver + shifted)
    return tallies[jax.random.permutation(jax.random.fold_in(rng, 2), number_of)]


def gaussian(rng, shape, deviation, reach, cuts=(), kind=jnp.bfloat16):
    drawn = deviation * jax.random.normal(rng, shape, jnp.float32)
    if cuts:
        drawn = drawn * block_levels(rng, shape, cuts, -0.22, 0.18)
    return jnp.clip(drawn, -reach, reach).astype(kind)


def setup_inputs(seed: int = 0) -> dict:
    key_list = jax.random.split(jax.random.key(seed), 12)
    segment_matrix = draw_segment_matrix(jax.random.fold_in(key_list[11], 71), 0)
    filled_sequence_segments = jax.vmap(lambda own: ragged_sizes(own, SER_DEV, TOK_DEV, MAXP, 2))(jax.random.split(key_list[1], N_DP)).reshape((N_DP, SER_DEV)).astype(jnp.int32)
    leading_filler_number = with_ends(jax.random.randint(key_list[2], (N_DP, SER_DEV), 0, 4), jax.random.fold_in(key_list[2], 1), 0, 3).astype(jnp.int32)
    segment_lifting_matrix = gaussian(key_list[3], (PATCH, MODEL_WIDTH), PATCH ** -0.5, 1.0, ((1, 16),))
    triple_projector_matrix = gaussian(key_list[4], (LAYERS, 3, MODEL_WIDTH, HEADS * HEAD), MODEL_WIDTH ** -0.5, 0.15625, ((2, 16), (3, 2)))
    mixer_exit_matrix = gaussian(key_list[5], (LAYERS, HEADS * HEAD, MODEL_WIDTH), (HEADS * HEAD // 4) ** -0.5, 0.3125, ((1, 2), (2, 16)))
    widen_matrix = gaussian(key_list[6], (LAYERS, MODEL_WIDTH, FF), MODEL_WIDTH ** -0.5, 0.15625, ((1, 16), (2, 2)))
    shrink_matrix = gaussian(key_list[7], (LAYERS, FF, MODEL_WIDTH), (FF // 2) ** -0.5, 0.25, ((1, 2), (2, 16)))
    normalizer_factors = jnp.clip(1.0 + 0.18 * jax.random.normal(key_list[8], (LAYERS, 2, MODEL_WIDTH), jnp.float32), 0.099609375, 1.8984375).astype(jnp.bfloat16)
    prediction_matrix = gaussian(key_list[9], (MODEL_WIDTH, HORIZON_STEPS), MODEL_WIDTH ** -0.5, 0.15625, ((0, 16), (1, 2)))
    prediction_sensitivity = gaussian(key_list[10], (SEGMENT_TOTAL, HORIZON_STEPS), 1.0, 6.0, ((0, 16), (1, 2)))
    return {"segment_matrix": segment_matrix, "filled_sequence_segments": filled_sequence_segments, "leading_filler_number": leading_filler_number, "segment_lifting_matrix": segment_lifting_matrix, "triple_projector_matrix": triple_projector_matrix, "mixer_exit_matrix": mixer_exit_matrix, "widen_matrix": widen_matrix, "shrink_matrix": shrink_matrix, "normalizer_factors": normalizer_factors, "prediction_matrix": prediction_matrix, "prediction_sensitivity": prediction_sensitivity}


EPS = 1e-06
FLOOR = 1.0
HIGH = lax.Precision.HIGHEST
NEG = -1e+30

@jax.custom_vjp
def low(v):
    return lax.optimization_barrier(v.astype(jnp.bfloat16)).astype(jnp.float32)

@jax.custom_vjp
def low_back(v):
    return v

def low_keep(v):
    return (low(v), None)

def low_pass(kept, grad):
    return (grad,)

def back_keep(v):
    return (v, None)

def back_low(kept, grad):
    return (low(grad),)
low.defvjp(low_keep, low_pass)
low_back.defvjp(back_keep, back_low)

def matmul(left, right):
    return jnp.dot(left, right, precision=HIGH)

def layout(counts, pads):
    rows = jnp.arange(TOK_DEV, dtype=jnp.int32)
    counts = counts.astype(jnp.int32)
    ends = jnp.cumsum(counts).astype(jnp.int32)
    starts = ends - counts
    first = starts + jnp.minimum(pads.astype(jnp.int32), counts - 1)
    series = lax.optimization_barrier(jnp.sum((starts[None, :] <= rows[:, None]).astype(jnp.int32), axis=1)) - 1
    series = series.astype(jnp.int32)
    member = series[:, None] == jnp.arange(SER_DEV, dtype=jnp.int32)[None, :]
    first_row = lax.optimization_barrier(jnp.sum(jnp.where(member, first[None, :], 0), axis=1)).astype(jnp.int32)
    genuine_segments = rows >= first_row
    place = (rows - first_row).astype(jnp.float32)
    return (series, first, genuine_segments, place)

def rms_norm(values, gain):
    return values * lax.rsqrt(lax.optimization_barrier(jnp.mean(values * values, axis=-1, keepdims=True)) + EPS) * gain

def rotate(values, place):
    half = values.shape[-1] // 2
    freq = jnp.exp(-jnp.arange(half).astype(jnp.float32) * (2.0 * math.log(10000.0) / values.shape[-1]))
    angle = place[:, None, None] * freq[None, None, :]
    cosine = jnp.cos(angle)
    sine = jnp.sin(angle)
    front = values[..., :half]
    back = values[..., half:]
    return jnp.concatenate([front * cosine - back * sine, back * cosine + front * sine], axis=-1)

def normalize(points, first, series, genuine_segments):
    firsts = points[first]
    mean = lax.optimization_barrier(jnp.mean(firsts, axis=1))
    centred = firsts - mean[:, None]
    spread = jnp.sqrt(lax.optimization_barrier(jnp.mean(centred * centred, axis=1)))
    sigma = jnp.maximum(spread, FLOOR)
    first_patch_mean = mean[series]
    first_patch_sigma = sigma[series]
    scaled = jnp.where(genuine_segments[:, None], (points - first_patch_mean[:, None]) / first_patch_sigma[:, None], 0.0)
    return (scaled, first_patch_mean, first_patch_sigma)

def attend_group(query, keys, values, series, genuine_segments):
    width = QBLOCK + KEYS_BACK
    lead = ((KEYS_BACK, 0), (0, 0), (0, 0))
    keys_pad = jnp.pad(keys, lead)
    values_pad = jnp.pad(values, lead)
    series_pad = jnp.concatenate([jnp.full((KEYS_BACK,), -1, jnp.int32), series.astype(jnp.int32)])
    real_pad = jnp.concatenate([jnp.zeros((KEYS_BACK,), bool), genuine_segments])
    scale = query.shape[-1] ** (-0.5)

    def one(index):
        start = (index * QBLOCK).astype(jnp.int32)
        query_blk = lax.dynamic_slice_in_dim(query, start, QBLOCK, 0)
        keys_win = lax.dynamic_slice_in_dim(keys_pad, start, width, 0)
        values_win = lax.dynamic_slice_in_dim(values_pad, start, width, 0)
        series_q = lax.dynamic_slice_in_dim(series_pad, start + KEYS_BACK, QBLOCK, 0)
        series_k = lax.dynamic_slice_in_dim(series_pad, start, width, 0)
        real_k = lax.dynamic_slice_in_dim(real_pad, start, width, 0)
        rows_q = start + jnp.arange(QBLOCK, dtype=jnp.int32)
        rows_k = start - KEYS_BACK + jnp.arange(width, dtype=jnp.int32)
        allowed = (series_q[:, None] == series_k[None, :]) & (rows_k[None, :] <= rows_q[:, None])
        allowed = allowed & (real_k[None, :] | (rows_k[None, :] == rows_q[:, None]))
        scores = jnp.einsum('qhd,khd->hqk', query_blk, keys_win, precision=HIGH) * scale
        scores = jnp.where(allowed[None], low_back(scores), NEG)
        top = lax.optimization_barrier(jnp.max(scores, axis=-1, keepdims=True))
        expd = jnp.exp(scores - top)
        probs = expd / lax.optimization_barrier(jnp.sum(expd, axis=-1, keepdims=True))
        return jnp.einsum('hqk,khd->qhd', low(probs), values_win, precision=HIGH)
    blocks = lax.map(jax.checkpoint(one), jnp.arange(TOK_DEV // QBLOCK, dtype=jnp.int32))
    return blocks.reshape(TOK_DEV, query.shape[1], query.shape[2])

def decoder_layer(residual, triple_projector_matrix, mixer_exit_matrix, widen_matrix, shrink_matrix, normalizer_factors, series, genuine_segments, place):
    normed = low(rms_norm(residual, normalizer_factors[0]))
    proj = low_back(jnp.einsum('td,cde->cte', normed, triple_projector_matrix, precision=HIGH))
    flat_shape = (SEGMENT_TOTAL, HEADS, HEAD)
    group_shape = (N_DP, TOK_DEV, HEADS, HEAD)
    query = low(rotate(proj[0].reshape(flat_shape), place)).reshape(group_shape)
    keys = low(rotate(proj[1].reshape(flat_shape), place)).reshape(group_shape)
    values = low(proj[2]).reshape(group_shape)
    attend = jax.checkpoint(attend_group)
    attended = lax.map(lambda parts: attend(parts[0], parts[1], parts[2], parts[3], parts[4]), (query, keys, values, series, genuine_segments))
    attended = low_back(low(attended.reshape(SEGMENT_TOTAL, HEADS * HEAD)))
    mid = residual + low_back(matmul(attended, mixer_exit_matrix))
    normed_ff = low(rms_norm(mid, normalizer_factors[1]))
    pre = low_back(matmul(normed_ff, widen_matrix))
    hidden = low(jax.nn.gelu(pre, approximate=True))
    return mid + low_back(matmul(hidden, shrink_matrix))

def reference(segment_matrix, filled_sequence_segments, leading_filler_number, segment_lifting_matrix, triple_projector_matrix, mixer_exit_matrix, widen_matrix, shrink_matrix, normalizer_factors, prediction_matrix, prediction_sensitivity):
    series, first, genuine_segments, place = jax.vmap(layout)(filled_sequence_segments, leading_filler_number)
    real_rows = genuine_segments.reshape(SEGMENT_TOTAL)
    place_rows = place.reshape(SEGMENT_TOTAL)

    def evaluate_model(points, embed, qkv_all, attn_all, up_all, down_all, gain_all, head):
        groups = points.reshape(N_DP, TOK_DEV, PATCH)
        scaled, first_patch_mean, first_patch_sigma = jax.vmap(normalize)(groups, first, series, genuine_segments)
        scaled = scaled.reshape(SEGMENT_TOTAL, PATCH)
        first_patch_mean = first_patch_mean.reshape(SEGMENT_TOTAL)
        first_patch_sigma = first_patch_sigma.reshape(SEGMENT_TOTAL)
        residual = low_back(matmul(low(scaled), embed))
        for layer in range(LAYERS):
            residual = decoder_layer(residual, qkv_all[layer], attn_all[layer], up_all[layer], down_all[layer], gain_all[layer], series, genuine_segments, place_rows)
        unscaled_input = low_back(matmul(low(residual), head))
        return jnp.where(real_rows[:, None], unscaled_input * first_patch_sigma[:, None] + first_patch_mean[:, None], 0.0)
    decimal_numbers = tuple((vector_entry.astype(jnp.float32) for vector_entry in (segment_matrix, segment_lifting_matrix, triple_projector_matrix, mixer_exit_matrix, widen_matrix, shrink_matrix, normalizer_factors, prediction_matrix)))
    predictions, reverse_mapping = jax.vjp(evaluate_model, *decimal_numbers)
    parameter_sensitivities = reverse_mapping(prediction_sensitivity.astype(jnp.float32))
    return (predictions, parameter_sensitivities[0], parameter_sensitivities[1], parameter_sensitivities[2], parameter_sensitivities[3], parameter_sensitivities[4], parameter_sensitivities[5], parameter_sensitivities[6], parameter_sensitivities[7])
```

```python
from functools import partial
import math

import jax
import jax.numpy as jnp
from jax import lax
from jax.experimental import pallas as pl
from jax.experimental.pallas import tpu as pltpu
from jax.sharding import PartitionSpec as P

HEAD = 80
LAYERS = 2
MAXP = 64
EPS = 1e-06
FLOOR = 1.0
HIGH = lax.Precision.HIGHEST
NEG = -1e30
F32 = jnp.float32
BF16 = jnp.bfloat16
VMEM_LIMIT = 40 * 1024 * 1024


class Moves:
    def __init__(self, n_dp):
        self.q = n_dp // 4
        self.n = n_dp

    def core(self, v):
        return lax.ppermute(v, "dp", [(i, i ^ 1) for i in range(self.n)])

    def x(self, v):
        return lax.ppermute(v, "dp", [(i, i ^ 2) for i in range(self.n)])

    def z(self, v, k):
        return lax.ppermute(v, "dp", [(i, (i + 4 * k) % self.n) for i in range(self.n)])

    def y(self, v):
        return lax.ppermute(v, "mp", [(0, 1), (1, 0)])


def after(value, *earlier):
    return lax.optimization_barrier((value,) + earlier)[0]


def cat(parts, axis):
    return parts[0] if len(parts) == 1 else jnp.concatenate(parts, axis=axis)


def gather_weights(mv, pairs):
    planes = []
    last = None
    for a, b in pairs:
        own = a[None] if b is None else jnp.stack([a, b])
        parts = [own]
        for k in range(1, mv.q):
            last = mv.z(own if last is None else after(own, last), k)
            parts.append(last)
        planes.append(cat(parts, 1))
    history = []

    def step(to_x, to_y):
        if len(history) >= 2:
            to_x, to_y = after((to_x, to_y), history[-2])
        history.append((mv.x(to_x), mv.y(to_y)))
        return history[-1]

    first = [None] * len(pairs)

    def one(i):
        a, b = planes[i][:1], planes[i][-1:]
        first[i] = step(a, b)

    result = []

    def two(i):
        a, b = planes[i][:1], planes[i][-1:]
        from_x, from_y = first[i]
        if pairs[i][1] is None:
            half = jnp.concatenate([jnp.concatenate([a, from_x], axis=1), jnp.concatenate([from_y, mv.x(from_y)], axis=1)])
        else:
            b_two, a_two = jnp.stack([b, from_y]), jnp.stack([a, from_x])
            b_far, a_far = step(b_two, a_two)
            rows = a.shape[1] * 2
            half = jnp.concatenate(
                [
                    jnp.concatenate([a, from_x], axis=1),
                    jnp.concatenate([a_far[0], a_far[1]], axis=1),
                    jnp.concatenate([b, b_far[0]], axis=1),
                    jnp.concatenate([from_y, b_far[1]], axis=1),
                ]
            )
        whole = jnp.concatenate([half, mv.core(half)], axis=1)
        result.append([whole[2 * j : 2 * j + 2] for j in range(whole.shape[0] // 2)])

    one(0)
    for i in range(len(pairs)):
        if i + 1 < len(pairs):
            one(i + 1)
        two(i)
    return result


class Scatter:
    def __init__(self, mv):
        self.mv = mv
        self.history = []
        self.cores = []
        self.waiting = None
        self.last = None
        self.done = []

    def step(self, to_x, to_y):
        if len(self.history) >= 2:
            if to_x is None:
                to_y = after(to_y, self.history[-2])
            else:
                to_x, to_y = after((to_x, to_y), self.history[-2])
        got = (None if to_x is None else self.mv.x(to_x), self.mv.y(to_y))
        self.history.append(got)
        return got

    def add(self, a, b):
        mv = self.mv
        grads = jnp.stack(a)[None] if b is None else jnp.stack([jnp.stack(a), jnp.stack(b)])
        half = grads.shape[2] // 2
        send = grads[:, :, half:]
        if len(self.cores) >= 2:
            send = after(send, self.cores[-2])
        got = mv.core(send)
        self.cores.append(got)
        summed = grads[:, :, :half] + got
        quarter = half // 2
        if b is None:
            _, from_y = self.step(None, summed[:, 1])
            entry = (summed[:, 0] + from_y, None)
        else:
            from_x, from_y = self.step(summed[1:, :, quarter:], summed[:1, 1])
            entry = (summed[:1, 0] + from_y, summed[1:, :, :quarter] + from_x)
        if self.waiting is not None:
            self.finish()
        self.waiting = entry

    def finish(self):
        mv = self.mv
        a, b = self.waiting
        self.waiting = None
        quarter = a.shape[1] // 2
        if b is None:
            total = a[:, :quarter] + mv.x(a[:, quarter:])
        else:
            from_x, from_y = self.step(a[:, quarter:], b[:, 1])
            total = jnp.concatenate([a[:, :quarter] + from_x, b[:, 0] + from_y])
        rows = quarter // mv.q
        parts = [total[:, k * rows : (k + 1) * rows] for k in range(mv.q)]
        out = parts[0].astype(F32)
        for k in range(1, mv.q):
            send = parts[k] if self.last is None else after(parts[k], self.last)
            self.last = mv.z(send, mv.q - k)
            out = out + self.last.astype(F32)
        self.done.append(out)


def head_windows(width):
    found = []
    for head in range(width // HEAD):
        low, high = head * HEAD, (head + 1) * HEAD
        found.append((low, high, low // 128 * 128, min(width, -(-high // 128) * 128)))
    return found


def in_head(low, high, start, stop):
    lane = lax.broadcasted_iota(jnp.int32, (1, stop - start), 1) + start
    return (lane >= low) & (lane < high)


def turn(values, cosine, ahead, behind):
    width = values.shape[-1]
    half = HEAD // 2
    return values * cosine + pltpu.roll(values, width - half, 1) * ahead + pltpu.roll(values, half, 1) * behind


def dot(a, b, dims):
    return lax.dot_general(a, b, (dims, ((), ())), preferred_element_type=F32)


def attend_kernel(q_ref, k_ref, v_ref, bias_ref, cos_ref, ahead_ref, behind_ref, out_ref, probs_ref, qr_ref, kr_ref, vr_ref):
    width = q_ref.shape[-1]
    cosine, ahead, behind = cos_ref[...], ahead_ref[...], behind_ref[...]
    qr_ref[0] = turn(q_ref[0], cosine, ahead, behind).astype(BF16)
    kr_ref[0] = turn(k_ref[0], cosine, ahead, behind).astype(BF16)
    vr_ref[0] = v_ref[0].astype(BF16)
    bias = bias_ref[...]
    scale = HEAD ** (-0.5)
    tiles = [None] * (width // 128)
    for head, (low, high, start, stop) in enumerate(head_windows(width)):
        mine = in_head(low, high, start, stop)
        query = jnp.where(mine, qr_ref[0, :, start:stop], 0)
        scores = dot(query, kr_ref[0, :, start:stop], ((1,), (1,))) * scale + bias
        top = jnp.max(scores, axis=-1, keepdims=True)
        grown = jnp.exp(scores - top)
        total = jnp.sum(grown, axis=-1, keepdims=True)
        probs = (grown / total).astype(BF16)
        probs_ref[0, head] = probs
        value = jnp.where(mine, vr_ref[0, :, start:stop], 0)
        part = dot(probs, value, ((1,), (0,)))
        for tile in range(start // 128, stop // 128):
            piece = part[:, tile * 128 - start : tile * 128 - start + 128]
            tiles[tile] = piece if tiles[tile] is None else tiles[tile] + piece
    for tile, total in enumerate(tiles):
        out_ref[0, :, tile * 128 : tile * 128 + 128] = total.astype(BF16)


def attend_forward(q, k, v, bias, tables):
    halves, rows, width = q.shape
    heads = width // HEAD
    block = pl.BlockSpec((1, rows, width), lambda i: (i, 0, 0))
    whole = pl.BlockSpec((rows, width), lambda i: (0, 0))
    shape = jax.ShapeDtypeStruct((halves, rows, width), BF16)
    return pl.pallas_call(
        attend_kernel,
        grid=(halves,),
        in_specs=[block] * 3 + [pl.BlockSpec((rows, rows), lambda i: (0, 0))] + [whole] * 3,
        out_specs=[block, pl.BlockSpec((1, heads, rows, rows), lambda i: (i, 0, 0, 0)), block, block, block],
        out_shape=[shape, jax.ShapeDtypeStruct((halves, heads, rows, rows), BF16), shape, shape, shape],
        compiler_params=pltpu.CompilerParams(vmem_limit_bytes=VMEM_LIMIT),
    )(q, k, v, bias, *tables)


def attend_back_kernel(g_ref, probs_ref, q_ref, k_ref, v_ref, cos_ref, ahead_ref, behind_ref, out_ref):
    width = q_ref.shape[-1]
    scale = HEAD ** (-0.5)
    count = width // 128
    tiles = [[None] * count for _ in range(3)]
    for head, (low, high, start, stop) in enumerate(head_windows(width)):
        mine = in_head(low, high, start, stop)
        grad = jnp.where(mine, g_ref[0, :, start:stop], 0)
        query = jnp.where(mine, q_ref[0, :, start:stop], 0)
        key = jnp.where(mine, k_ref[0, :, start:stop], 0)
        probs_low = probs_ref[0, head]
        probs = probs_low.astype(F32)
        grad_probs = dot(grad, v_ref[0, :, start:stop], ((1,), (1,)))
        delta = jnp.sum(grad_probs * probs, axis=-1, keepdims=True)
        grad_scores = (probs * (grad_probs - delta)).astype(BF16)
        found = (
            dot(grad_scores, key, ((1,), (0,))),
            dot(grad_scores, query, ((0,), (0,))),
            dot(probs_low, grad, ((0,), (0,))),
        )
        for which, part in enumerate(found):
            for tile in range(start // 128, stop // 128):
                piece = part[:, tile * 128 - start : tile * 128 - start + 128]
                tiles[which][tile] = piece if tiles[which][tile] is None else tiles[which][tile] + piece
    cosine, ahead, behind = cos_ref[...], ahead_ref[...], behind_ref[...]
    for which in range(2):
        whole = jnp.concatenate(tiles[which], axis=1) * scale
        out_ref[which, 0] = turn(whole, cosine, -ahead, -behind).astype(BF16)
    out_ref[2, 0] = jnp.concatenate(tiles[2], axis=1).astype(BF16)


def attend_backward(grad, probs, q, k, v, tables):
    halves, rows, width = q.shape
    heads = width // HEAD
    block = pl.BlockSpec((1, rows, width), lambda i: (i, 0, 0))
    whole = pl.BlockSpec((rows, width), lambda i: (0, 0))
    return pl.pallas_call(
        attend_back_kernel,
        grid=(halves,),
        in_specs=[block, pl.BlockSpec((1, heads, rows, rows), lambda i: (i, 0, 0, 0)), block, block, block] + [whole] * 3,
        out_specs=pl.BlockSpec((3, 1, rows, width), lambda i: (0, i, 0, 0)),
        out_shape=jax.ShapeDtypeStruct((3, halves, rows, width), BF16),
        compiler_params=pltpu.CompilerParams(vmem_limit_bytes=VMEM_LIMIT),
    )(grad, probs, q, k, v, *tables)


def rms_norm(values, gain):
    return values * lax.rsqrt(jnp.mean(values * values, axis=-1, keepdims=True) + EPS) * gain


def into(values, weight):
    return jnp.einsum("td,hde->hte", values, weight, preferred_element_type=F32)


def out_of(values, weight):
    return jnp.einsum("hte,hde->td", values, weight, preferred_element_type=F32)


def weight_grad(values, grads):
    return tuple(
        jnp.einsum("td,te->de", values, grads[half], preferred_element_type=F32).astype(BF16) for half in range(2)
    )


def layer_forward(residual, weights, gain, bias, tables):
    wq, wk, wv, wo, wu, wd = weights
    normed = rms_norm(residual, gain[0]).astype(BF16)
    attended, probs, query, keys, values = attend_forward(into(normed, wq), into(normed, wk), into(normed, wv), bias, tables)
    mid = residual + out_of(attended, wo)
    normed_ff = rms_norm(mid, gain[1]).astype(BF16)
    pre = into(normed_ff, wu)
    hidden = jax.nn.gelu(pre, approximate=True).astype(BF16)
    result = mid + out_of(hidden, wd)
    return result, (residual, normed, query, keys, values, probs, attended, mid, normed_ff, pre, hidden)


def layer_backward(grad_res, weights, gain, saved, tables, scatter):
    wq, wk, wv, wo, wu, wd = weights
    residual, normed, query, keys, values, probs, attended, mid, normed_ff, pre, hidden = saved
    grad_low = grad_res.astype(BF16)
    grad_hidden = into(grad_low, wd)
    down = tuple(jnp.einsum("td,te->de", grad_low, hidden[h], preferred_element_type=F32).astype(BF16) for h in range(2))
    grad_pre = jax.vjp(partial(jax.nn.gelu, approximate=True), pre)[1](grad_hidden)[0].astype(BF16)
    scatter.add(down, weight_grad(normed_ff, grad_pre))
    grad_nf = out_of(grad_pre, wu)
    grad_mid_norm, gain_two = jax.vjp(rms_norm, mid, gain[1])[1](grad_nf)
    grad_mid = grad_res + grad_mid_norm
    mid_low = grad_mid.astype(BF16)
    grad_att = into(mid_low, wo).astype(BF16)
    attn = weight_grad(mid_low, attended)
    grad_proj = attend_backward(grad_att, probs, query, keys, values, tables)
    scatter.add(attn, weight_grad(normed, grad_proj[2]))
    scatter.add(weight_grad(normed, grad_proj[0]), weight_grad(normed, grad_proj[1]))
    grad_normed = out_of(grad_proj[0], wq) + out_of(grad_proj[1], wk) + out_of(grad_proj[2], wv)
    grad_in_norm, gain_one = jax.vjp(rms_norm, residual, gain[0])[1](grad_normed)
    return grad_mid + grad_in_norm, (gain_one, gain_two)


def on_device(
    segment_matrix,
    filled_sequence_segments,
    leading_filler_number,
    segment_lifting_matrix,
    triple_projector_matrix,
    mixer_exit_matrix,
    widen_matrix,
    shrink_matrix,
    normalizer_factors,
    prediction_matrix,
    prediction_sensitivity,
    n_dp,
):
    mv = Moves(n_dp)
    tokens, patch = segment_matrix.shape
    window = tokens // 2 + MAXP // 2
    skipped = tokens - window
    second = lax.axis_index("mp") == 1

    def mine(values):
        return jnp.where(second, values[skipped:], values[:window])

    def other(values):
        return jnp.where(second, values[:window], values[skipped:])

    def joined(own, got, cut):
        front, back = jnp.where(second, got, own), jnp.where(second, own, got)
        rows = skipped + jnp.arange(window - skipped, dtype=jnp.int32)
        shared = jnp.where((rows < cut)[:, None], front[skipped:], back[: window - skipped])
        return jnp.concatenate([front[:skipped], shared, back[window - skipped :]])

    small = jnp.concatenate(
        [segment_lifting_matrix.T, normalizer_factors.reshape(2 * LAYERS, -1).T], axis=1
    )
    small = cat([small] + [mv.z(small, k) for k in range(1, mv.q)], 0)
    small = jnp.concatenate([small, mv.x(small)])
    small = jnp.concatenate([small, mv.core(small)])
    embed = small[:, :patch]
    gains = small[:, patch:].T.astype(F32).reshape(LAYERS, 2, -1)
    sens_other = mv.y(other(prediction_sensitivity))

    pairs = []
    for layer in range(LAYERS):
        q, k, v = (triple_projector_matrix[layer, c] for c in range(3))
        pairs += [(q, k), (v, mixer_exit_matrix[layer].T), (widen_matrix[layer], shrink_matrix[layer].T)]
    pairs.append((prediction_matrix, None))
    gathered = gather_weights(mv, pairs)
    layers = [sum(gathered[3 * layer : 3 * layer + 3], []) for layer in range(LAYERS)]
    head = gathered[-1][0]

    counts, pads = filled_sequence_segments[0], leading_filler_number[0]
    ends = jnp.cumsum(counts)
    starts = ends - counts
    first = starts + jnp.minimum(pads, counts - 1)
    cut = jnp.max(jnp.where(ends <= window, ends, 0))
    rows = jnp.where(second, skipped, 0) + jnp.arange(window, dtype=jnp.int32)
    begun = starts[None, :] <= rows[:, None]
    start_row = jnp.max(jnp.where(begun, starts[None, :], 0), axis=1)
    first_row = jnp.max(jnp.where(begun, first[None, :], 0), axis=1)
    real = rows >= first_row
    place = (rows - first_row).astype(F32)
    valid = jnp.where(second, rows >= cut, rows < cut)
    counted = real & valid
    allowed = (start_row[:, None] == start_row[None, :]) & (rows[None, :] <= rows[:, None])
    allowed = allowed & (real[None, :] | (rows[None, :] == rows[:, None]))
    bias = jnp.where(allowed, 0.0, NEG).astype(F32)
    is_first = (first_row[:, None] == rows[None, :]).astype(F32)

    half = HEAD // 2
    width = triple_projector_matrix.shape[3]
    freq = jnp.exp(-jnp.arange(half).astype(F32) * (2.0 * math.log(10000.0) / HEAD))
    angle = place[:, None] * freq[None, :]
    cosine, sine, none = jnp.cos(angle), jnp.sin(angle), jnp.zeros((window, half), F32)
    heads = width // HEAD
    tables = (
        jnp.tile(cosine, (1, 2 * heads)),
        jnp.tile(jnp.concatenate([-sine, none], axis=1), (1, heads)),
        jnp.tile(jnp.concatenate([none, sine], axis=1), (1, heads)),
    )

    points = mine(segment_matrix)
    firsts = jnp.dot(is_first, points, precision=HIGH)
    mean = jnp.mean(firsts, axis=1, keepdims=True)
    centred = firsts - mean
    spread = jnp.sqrt(jnp.mean(centred * centred, axis=1, keepdims=True))
    sigma = jnp.maximum(spread, FLOOR)
    scaled_low = jnp.where(real[:, None], (points - mean) / sigma, 0.0).astype(BF16)

    residual = jnp.einsum("tp,dp->td", scaled_low, embed, preferred_element_type=F32)
    saved = []
    for layer in range(LAYERS):
        residual, kept = layer_forward(residual, layers[layer], gains[layer], bias, tables)
        saved.append(kept)
    final_low = residual.astype(BF16)
    raw = into(final_low, head)
    predictions = jnp.where(real[:, None], raw * sigma + mean, 0.0)
    sens = jnp.stack([mine(prediction_sensitivity), sens_other]).astype(F32)
    cot = jnp.where(counted[:, None], sens, 0.0)
    grad_raw = (cot * sigma).astype(BF16)

    scatter = Scatter(mv)
    scatter.add(weight_grad(final_low, grad_raw), None)
    grad_res = out_of(grad_raw, head)
    mean_term = jnp.sum(cot, axis=(0, 2))[:, None]
    sigma_term = jnp.sum(cot * raw, axis=(0, 2))[:, None]
    predictions = joined(predictions[0], mv.y(predictions[1].astype(BF16)).astype(F32), cut)

    gain_grads = [None] * LAYERS
    for layer in reversed(range(LAYERS)):
        grad_res, gain_grads[layer] = layer_backward(grad_res, layers[layer], gains[layer], saved[layer], tables, scatter)
    grad_low = grad_res.astype(BF16)
    grad_scaled = jnp.einsum("td,dp->tp", grad_low, embed, preferred_element_type=F32)
    embed_term = jnp.einsum("td,tp->dp", grad_low, scaled_low, preferred_element_type=F32)

    grad_scaled = jnp.where(real[:, None], grad_scaled, 0.0)
    mean_row = mean_term - jnp.sum(grad_scaled, axis=1, keepdims=True) / sigma
    sigma_row = sigma_term - jnp.sum(grad_scaled * (points - mean), axis=1, keepdims=True) / (sigma * sigma)
    sums = lax.dot_general(
        is_first, jnp.concatenate([mean_row, sigma_row], axis=1), (((0,), (0,)), ((), ())), precision=HIGH
    )
    pull = jnp.where(spread > FLOOR, (points - mean) / jnp.maximum(spread, FLOOR), 0.0)
    patches = grad_scaled / sigma + sums[:, :1] / patch + sums[:, 1:] * pull / patch
    patches_grad = joined(patches, mv.y(patches), cut)

    tail = jnp.concatenate([embed_term] + [g[:, None] for pair in gain_grads for g in pair], axis=1)
    n = tail.shape[0]
    tail = tail[: n // 2] + mv.core(tail[n // 2 :])
    tail = tail[: n // 4] + mv.x(tail[n // 4 :])
    tail = tail + mv.y(tail)
    n = tail.shape[0] // mv.q
    tail_out = tail[:n]
    for k in range(1, mv.q):
        tail_out = tail_out + mv.z(tail[k * n : (k + 1) * n], mv.q - k)
    w_in_grad = tail_out[:, :patch].T
    gains_grad = tail_out[:, patch:].T.reshape(LAYERS, 2, -1)

    scatter.finish()
    done = scatter.done
    qkv, attn, up, down = [None] * LAYERS, [None] * LAYERS, [None] * LAYERS, [None] * LAYERS
    at = 1
    for layer in reversed(range(LAYERS)):
        down[layer], up[layer] = done[at][0].T, done[at][1]
        attn[layer] = done[at + 1][0].T
        qkv[layer] = jnp.stack([done[at + 2][0], done[at + 2][1], done[at + 1][1]])
        at += 3
    return (
        predictions,
        patches_grad,
        w_in_grad,
        jnp.stack(qkv),
        jnp.stack(attn),
        jnp.stack(up),
        jnp.stack(down),
        gains_grad,
        done[0][0],
    )


def solution(mesh):
    placed = (
        P("dp", None),
        P("dp", None),
        P("dp", None),
        P(None, "dp"),
        P(None, None, "dp", "mp"),
        P(None, "mp", "dp"),
        P(None, "dp", "mp"),
        P(None, "mp", "dp"),
        P(None, None, "dp"),
        P("dp", "mp"),
        P("dp", "mp"),
    )
    return jax.shard_map(
        partial(on_device, n_dp=mesh.shape["dp"]),
        mesh=mesh,
        in_specs=placed,
        out_specs=(
            P("dp", "mp"),
            P("dp", None),
            P(None, "dp"),
            P(None, None, "dp", "mp"),
            P(None, "mp", "dp"),
            P(None, "dp", "mp"),
            P(None, "mp", "dp"),
            P(None, None, "dp"),
            P("dp", "mp"),
        ),
        check_vma=False,
    )
```

```python
from functools import partial
import math

import jax
import jax.numpy as jnp
from jax import lax
from jax.experimental import pallas as pl
from jax.experimental.pallas import tpu as pltpu
from jax.sharding import PartitionSpec as P

HEAD = 80
LAYERS = 2
MAXP = 64
EPS = 1e-06
FLOOR = 1.0
HIGH = lax.Precision.HIGHEST
NEG = -1e30
F32 = jnp.float32
BF16 = jnp.bfloat16
VMEM_LIMIT = 48 * 1024 * 1024
LAG = 2


class Moves:
    def __init__(self, n_dp):
        self.q = n_dp // 4
        self.n = n_dp

    def core(self, v):
        return lax.ppermute(v, "dp", [(i, i ^ 1) for i in range(self.n)])

    def x(self, v):
        return lax.ppermute(v, "dp", [(i, i ^ 2) for i in range(self.n)])

    def z(self, v, k):
        return lax.ppermute(v, "dp", [(i, (i + 4 * k) % self.n) for i in range(self.n)])

    def y(self, v):
        return lax.ppermute(v, "mp", [(0, 1), (1, 0)])


def after(value, *earlier):
    return lax.optimization_barrier((value,) + earlier)[0]


def cat(parts, axis):
    return parts[0] if len(parts) == 1 else jnp.concatenate(parts, axis=axis)


def total(*parts):
    found = parts[0].astype(F32)
    for part in parts[1:]:
        found = found + part.astype(F32)
    return found


class Scatter:
    def __init__(self, mv):
        self.mv = mv
        self.history = []
        self.cores = []
        self.waiting = None
        self.last = None
        self.done = []
        self.second = []

    def step(self, to_x, to_y):
        if len(self.history) >= 2:
            if to_x is None:
                to_y = after(to_y, self.history[-2])
            else:
                to_x, to_y = after((to_x, to_y), self.history[-2])
        got = (None if to_x is None else self.mv.x(to_x), self.mv.y(to_y))
        self.history.append(got)
        return got

    def add(self, a, b):
        mv = self.mv
        a_keep, a_send = a
        a_got = mv.core(a_send)
        self.cores.append(a_got)
        to_y = total(a_keep[1], a_got[1]).astype(BF16)
        if b is None:
            _, from_y = self.step(None, to_y)
            self.second.append(from_y)
            entry = ((a_keep[0], a_got[0], from_y), None)
        else:
            b_keep, b_send = b
            b_got = mv.core(b_send)
            half = b_keep.shape[1] // 2
            to_x = total(b_keep[:, half:], b_got[:, half:]).astype(BF16)
            from_x, from_y = self.step(to_x, to_y)
            self.second.append((from_x, from_y))
            entry = ((a_keep[0], a_got[0], from_y), (b_keep[:, :half], b_got[:, :half], from_x))
        if self.waiting is not None:
            self.finish()
        self.waiting = entry

    def finish(self):
        mv = self.mv
        a, b = self.waiting
        self.waiting = None
        half = a[0].shape[0] // 2
        to_x = total(*[part[half:] for part in a]).astype(BF16)
        if b is None:
            from_x = mv.x(to_x)
            found = [total(*[part[:half] for part in a], from_x)]
        else:
            from_x, from_y = self.step(to_x, total(*[part[1] for part in b]).astype(BF16))
            found = [total(*[part[:half] for part in a], from_x), total(*[part[0] for part in b], from_y)]
        rows = half // mv.q
        out = jnp.stack([part[:rows] for part in found])
        sends = [jnp.stack([part[k * rows : (k + 1) * rows].astype(BF16) for part in found]) for k in range(1, mv.q)]
        if self.last is not None:
            sends = after(sends, self.last)
        self.last = [mv.z(send, mv.q - k) for k, send in enumerate(sends, 1)]
        for got in self.last:
            out = out + got.astype(F32)
        self.done.append(out)


def dot(a, b, dims):
    return lax.dot_general(a, b, (dims, ((), ())), preferred_element_type=F32)


class Matrix:
    def __init__(self, halves):
        self.halves = halves
        self.rows, self.cols = halves[0][0][0].shape[-2:]

    def built(self, order):
        found = []
        for half in self.halves:
            blocks = []
            for place, (array, shift, index) in enumerate(half):
                block = lax.dynamic_index_in_dim(array, order[place] >> shift, 0, keepdims=False)
                blocks.append(block[index])
            found.append(jnp.concatenate(blocks))
        return jnp.stack(found)


def run_kernel(body, arrays, matrices, outs, order):
    sources, plan, shapes = [], [], []

    def source(array):
        for i, known in enumerate(sources):
            if known is array:
                return i
        sources.append(array)
        return len(sources) - 1

    for which, matrix in enumerate(matrices):
        if matrix.rows % 16:
            found = matrix.built(order)
            plan.append((which, None, source(found), None, None))
            shapes.append(found.shape)
            continue
        for half in range(2):
            for place, (array, shift, index) in enumerate(matrix.halves[half]):
                plan.append((which, (half, pl.ds(place * matrix.rows, matrix.rows)), source(array), (place, shift), index))
        shapes.append((2, len(matrix.halves[0]) * matrix.rows, matrix.cols))
    n_in, n_out = len(arrays), len(outs)
    n_all = n_in + 1 + len(sources)

    def kernel(*refs):
        inputs, order_ref, parts = refs[:n_in], refs[n_in], refs[n_in + 1 : n_all]
        outputs, scratch = refs[n_all : n_all + n_out], refs[n_all + n_out :]
        buffers, sems = scratch[:-1], scratch[-1]
        copies = [[] for _ in matrices]
        for number, (which, target, at, pick, index) in enumerate(plan):
            if target is None:
                copy = pltpu.make_async_copy(parts[at], buffers[which], sems.at[number])
            else:
                device = lax.shift_right_logical(order_ref[pick[0]], pick[1])
                copy = pltpu.make_async_copy(parts[at].at[(device,) + index], buffers[which].at[target], sems.at[number])
            copy.start()
            copies[which].append(copy)

        def weight(which):
            def ready():
                for copy in copies[which]:
                    copy.wait()
                return buffers[which]

            return ready

        body(inputs, [weight(which) for which in range(len(matrices))], outputs, order_ref)

    vmem = pl.BlockSpec(memory_space=pltpu.VMEM)
    return pl.pallas_call(
        kernel,
        in_specs=[vmem] * n_in
        + [pl.BlockSpec(memory_space=pltpu.SMEM)]
        + [pl.BlockSpec(memory_space=pl.ANY)] * len(sources),
        out_specs=[vmem] * n_out,
        out_shape=[jax.ShapeDtypeStruct(dims, kind) for dims, kind in outs],
        scratch_shapes=[pltpu.VMEM(dims, BF16) for dims in shapes] + [pltpu.SemaphoreType.DMA((max(1, len(plan)),))],
        compiler_params=pltpu.CompilerParams(vmem_limit_bytes=VMEM_LIMIT),
        cost_estimate=pl.CostEstimate(flops=0, bytes_accessed=0, transcendentals=0),
    )(*arrays, order, *sources)


def head_windows(width):
    found = []
    for head in range(width // HEAD):
        low, high = head * HEAD, (head + 1) * HEAD
        found.append((low, high, low // 128 * 128, min(width, -(-high // 128) * 128)))
    return found


def in_head(low, high, start, stop):
    lane = lax.broadcasted_iota(jnp.int32, (1, stop - start), 1) + start
    return (lane >= low) & (lane < high)


def turn(values, cosine, ahead, behind):
    width = values.shape[-1]
    half = HEAD // 2
    return values * cosine + pltpu.roll(values, width - half, 1) * ahead + pltpu.roll(values, half, 1) * behind


def put(tiles, part, start, stop):
    for tile in range(start // 128, stop // 128):
        piece = part[:, tile * 128 - start : tile * 128 - start + 128]
        tiles[tile] = piece if tiles[tile] is None else tiles[tile] + piece


def gelu_parts(v):
    inner = math.sqrt(2.0 / math.pi) * (v + 0.044715 * (v * v * v))
    return jnp.tanh(inner)


def gelu_slope(v):
    tanh = gelu_parts(v)
    inner = math.sqrt(2.0 / math.pi) * (1.0 + 3.0 * 0.044715 * (v * v))
    return 0.5 * (1.0 + tanh) + 0.5 * v * (1.0 - tanh * tanh) * inner


def scale_of(values):
    return lax.rsqrt(jnp.mean(values * values, axis=-1, keepdims=True) + EPS)


def norm_back(values, gain, grad):
    scale = scale_of(values)
    plain = values * scale
    pushed = grad * gain
    back = scale * (pushed - plain * jnp.mean(pushed * plain, axis=-1, keepdims=True))
    return back, jnp.sum(grad * plain, axis=0, keepdims=True)


def split_grad(sink, half, values, grads):
    found = dot(values, grads, ((0,), (0,))).astype(BF16)
    if len(sink) == 2:
        keep, send = sink
        rows = keep.shape[1]
        keep[half] = found[:rows]
        send[half] = found[rows:]
    else:
        out, matrix, order = sink
        rows = out.shape[3]
        for place in range(out.shape[0]):
            out[order[place], half, matrix] = found[place * rows : (place + 1) * rows]


def project_body(inputs, weights, outputs, order):
    residual, gain, cosine, ahead, behind = inputs
    normed_out, q_out, k_out = outputs
    values = residual[...]
    normed = (values * scale_of(values) * gain[...]).astype(BF16)
    normed_out[...] = normed
    tables = (cosine[...], ahead[...], behind[...])
    for weight, out in zip(weights, (q_out, k_out)):
        matrix = weight()
        for half in range(2):
            out[half] = turn(dot(normed, matrix[half], ((1,), (0,))), *tables).astype(BF16)


def attend_body(inputs, weights, outputs, order):
    residual, normed, query, key, bias_ref = inputs
    mid_out, value_out, probs_out, attended_out = outputs
    width = query.shape[-1]
    scale = HEAD ** (-0.5)
    bias = bias_ref[...]
    matrix = weights[0]()
    for half in range(2):
        value_out[half] = dot(normed[...], matrix[half], ((1,), (0,))).astype(BF16)
    for half in range(2):
        tiles = [None] * (width // 128)
        for head, (low, high, start, stop) in enumerate(head_windows(width)):
            mine = in_head(low, high, start, stop)
            scores = dot(jnp.where(mine, query[half, :, start:stop], 0), key[half, :, start:stop], ((1,), (1,)))
            scores = scores * scale + bias
            grown = jnp.exp(scores - jnp.max(scores, axis=-1, keepdims=True))
            probs = (grown / jnp.sum(grown, axis=-1, keepdims=True)).astype(BF16)
            probs_out[half, head] = probs
            put(tiles, dot(probs, jnp.where(mine, value_out[half, :, start:stop], 0), ((1,), (0,))), start, stop)
        for tile, found in enumerate(tiles):
            attended_out[half, :, tile * 128 : tile * 128 + 128] = found.astype(BF16)
    matrix = weights[1]()
    mid = residual[...]
    for half in range(2):
        mid = mid + dot(attended_out[half], matrix[half], ((1,), (1,)))
    mid_out[...] = mid


def widen_body(inputs, weights, outputs, order):
    mid_ref, gain = inputs
    result_out, normed_out, pre_out, hidden_out = outputs
    mid = mid_ref[...]
    normed = (mid * scale_of(mid) * gain[...]).astype(BF16)
    normed_out[...] = normed
    matrix = weights[0]()
    for half in range(2):
        pre = dot(normed, matrix[half], ((1,), (0,)))
        pre_out[half] = pre
        hidden_out[half] = (0.5 * pre * (1.0 + gelu_parts(pre))).astype(BF16)
    matrix = weights[1]()
    for half in range(2):
        mid = mid + dot(hidden_out[half], matrix[half], ((1,), (1,)))
    result_out[...] = mid


def widen_back(grad, inputs, weights, outputs, down_sink, up_sink):
    hidden, pre, normed, mid, gain = inputs
    grad_out, gain_out = outputs
    low = grad.astype(BF16)
    down = weights[0]()
    back = None
    pushed = []
    for half in range(2):
        grad_hidden = dot(low, down[half], ((1,), (0,)))
        pushed.append((gelu_slope(pre[half]) * grad_hidden).astype(BF16))
        split_grad(down_sink, half, low, hidden[half])
    up = weights[1]()
    for half in range(2):
        split_grad(up_sink, half, normed[...], pushed[half])
        found = dot(pushed[half], up[half], ((1,), (1,)))
        back = found if back is None else back + found
    back, gain_out[...] = norm_back(mid[...], gain[...], back)
    grad_out[...] = grad + back


def head_body(inputs, weights, outputs, order):
    residual, sens_own, sens_other, real_ref, counted_ref, mean_ref, sigma_ref = inputs[:7]
    own_out, other_out, mean_out, sigma_out, grad_out, gain_out, weight_out = outputs
    final = residual[...].astype(BF16)
    real, counted = real_ref[...] > 0, counted_ref[...] > 0
    mean, sigma = mean_ref[...], sigma_ref[...]
    matrix = weights[0]()
    grad = mean_sum = sigma_sum = None
    for half, (sens, out) in enumerate(((sens_own, own_out), (sens_other, other_out))):
        raw = dot(final, matrix[half], ((1,), (0,)))
        out[...] = jnp.where(real, raw * sigma + mean, 0.0).astype(out.dtype)
        cot = jnp.where(counted, sens[...].astype(F32), 0.0)
        graw = (cot * sigma).astype(BF16)
        split_grad((weight_out, 0, order), half, final, graw)
        back = dot(graw, matrix[half], ((1,), (1,)))
        parts = (back, jnp.sum(cot, axis=1, keepdims=True), jnp.sum(cot * raw, axis=1, keepdims=True))
        grad, mean_sum, sigma_sum = parts if half == 0 else (grad + parts[0], mean_sum + parts[1], sigma_sum + parts[2])
    mean_out[...] = mean_sum
    sigma_out[...] = sigma_sum
    widen_back(grad, inputs[7:], weights[1:], (grad_out, gain_out), (weight_out, 1, order), (weight_out, 2, order))


def widen_back_body(inputs, weights, outputs, order):
    grad_out, gain_out, *sinks = outputs
    widen_back(inputs[0][...], inputs[1:], weights, (grad_out, gain_out), sinks[:2], sinks[2:])


def attend_back_body(inputs, weights, outputs, order):
    grad_ref, attended, probs_ref, query_ref, key_ref, value_ref, normed, cosine, ahead, behind = inputs
    proj_out, *sinks = outputs
    if len(sinks) == 1:
        attn_sink, value_sink = (sinks[0], 0, order), (sinks[0], 1, order)
    else:
        attn_sink, value_sink = sinks[:2], sinks[2:]
    width = query_ref.shape[-1]
    scale = HEAD ** (-0.5)
    low = grad_ref[...].astype(BF16)
    matrix = weights[0]()
    tables = (cosine[...], -ahead[...], -behind[...])
    for half in range(2):
        grad_att = dot(low, matrix[half], ((1,), (0,))).astype(BF16)
        split_grad(attn_sink, half, low, attended[half])
        tiles = [[None] * (width // 128) for _ in range(3)]
        for head, (first, end, start, stop) in enumerate(head_windows(width)):
            mine = in_head(first, end, start, stop)
            grad = jnp.where(mine, grad_att[:, start:stop], 0)
            query = jnp.where(mine, query_ref[half, :, start:stop], 0)
            key = jnp.where(mine, key_ref[half, :, start:stop], 0)
            probs_low = probs_ref[half, head]
            probs = probs_low.astype(F32)
            grad_probs = dot(grad, value_ref[half, :, start:stop], ((1,), (1,)))
            delta = jnp.sum(grad_probs * probs, axis=-1, keepdims=True)
            grad_scores = (probs * (grad_probs - delta)).astype(BF16)
            put(tiles[0], dot(grad_scores, key, ((1,), (0,))), start, stop)
            put(tiles[1], dot(grad_scores, query, ((0,), (0,))), start, stop)
            put(tiles[2], dot(probs_low, grad, ((0,), (0,))), start, stop)
        for which in range(2):
            proj_out[which, half] = turn(jnp.concatenate(tiles[which], axis=1) * scale, *tables).astype(BF16)
        proj_out[2, half] = jnp.concatenate(tiles[2], axis=1).astype(BF16)
        split_grad(value_sink, half, normed[...], proj_out[2, half])


def project_back_body(inputs, weights, outputs, order):
    grad_ref, proj, normed, residual, gain = inputs
    grad_out, gain_out, *sinks = outputs
    for half in range(2):
        split_grad(sinks[:2], half, normed[...], proj[0, half])
        split_grad(sinks[2:], half, normed[...], proj[1, half])
    back = None
    for which in range(3):
        matrix = weights[which]()
        for half in range(2):
            found = dot(proj[which, half], matrix[half], ((1,), (1,)))
            back = found if back is None else back + found
    back, gain_out[...] = norm_back(residual[...], gain[...], back)
    grad_out[...] = grad_ref[...] + back


def layer_forward(residual, weights, gain, bias, tables, order, width):
    pairs = weights if callable(weights) else lambda pair, gate: weights[2 * pair : 2 * pair + 2]
    rows, features = residual.shape
    halves, wide = (2, rows, width), (rows, features)
    wq, wk = pairs(0, None)
    wv, wo = pairs(1, None)
    normed, q, k = run_kernel(
        project_body, (residual, gain[:1], *tables), (wq, wk), [(wide, BF16), (halves, BF16), (halves, BF16)], order
    )
    mid, v, probs, attended = run_kernel(
        attend_body,
        (residual, normed, q, k, bias),
        (wv, wo),
        [(wide, F32), (halves, BF16), ((2, width // HEAD, rows, rows), BF16), (halves, BF16)],
        order,
    )
    wu, wd = pairs(2, mid)
    result, normed_ff, pre, hidden = run_kernel(
        widen_body, (mid, gain[1:]), (wu, wd), [(wide, F32), (wide, BF16), (halves, F32), (halves, BF16)], order
    )
    return result, (residual, normed, q, k, v, probs, attended, mid, normed_ff, pre, hidden), (wq, wk, wv, wo, wu, wd)


def attend_backward(grad, wo, saved, tables, order, blocks):
    _, normed, q, k, v, probs, attended = saved[:7]
    features, (_, rows, width) = normed.shape[1], q.shape
    grads = [((2, features // 2, width), BF16)] * 4 if blocks is None else [(blocks, BF16)]
    return run_kernel(
        attend_back_body,
        (grad, attended, probs, q, k, v, normed, *tables),
        (wo,),
        [((3, 2, rows, width), BF16)] + grads,
        order,
    )


def project_backward(grad, proj, weights, gain, saved, order):
    residual, normed = saved[:2]
    rows, features = residual.shape
    weight = ((2, features // 2, proj.shape[-1]), BF16)
    return run_kernel(
        project_back_body,
        (grad, proj, normed, residual, gain[:1]),
        weights[:3],
        [((rows, features), F32), ((1, features), F32)] + [weight] * 4,
        order,
    )


def on_device(
    segment_matrix,
    filled_sequence_segments,
    leading_filler_number,
    segment_lifting_matrix,
    triple_projector_matrix,
    mixer_exit_matrix,
    widen_matrix,
    shrink_matrix,
    normalizer_factors,
    prediction_matrix,
    prediction_sensitivity,
    n_dp,
):
    mv = Moves(n_dp)
    tokens, patch = segment_matrix.shape
    window = tokens // 2 + MAXP // 2
    skipped = tokens - window
    second = lax.axis_index("mp") == 1

    def mine(values):
        return jnp.where(second, values[skipped:], values[:window])

    def other(values):
        return jnp.where(second, values[:window], values[skipped:])

    def joined(own, got, cut):
        front, back = jnp.where(second, got, own), jnp.where(second, own, got)
        rows = skipped + jnp.arange(window - skipped, dtype=jnp.int32)
        shared = jnp.where((rows < cut)[:, None], front[skipped:], back[: window - skipped])
        return jnp.concatenate([front[:skipped], shared, back[window - skipped :]])

    small = jnp.concatenate(
        [segment_lifting_matrix.T, normalizer_factors.reshape(2 * LAYERS, -1).T], axis=1
    )
    small = cat([small] + [mv.z(small, k) for k in range(1, mv.q)], 0)
    small = jnp.concatenate([small, mv.x(small)])
    small = jnp.concatenate([small, mv.core(small)])
    embed = small[:, :patch]
    gains = small[:, patch:].T.astype(F32).reshape(LAYERS, 2, -1)
    sens_other = mv.y(other(prediction_sensitivity))

    def blocks_of(layer):
        qkv = [triple_projector_matrix[layer, c] for c in range(3)]
        return qkv + [mixer_exit_matrix[layer].T, widen_matrix[layer], shrink_matrix[layer].T]

    me = lax.axis_index("dp")
    place = jnp.arange(n_dp, dtype=jnp.int32)
    bits, behind = place // mv.q, place % mv.q
    order = ((me // 4 - behind) % mv.q * 4 + me % 4) ^ (2 * (bits % 2)) ^ (bits // 2)

    first_own = lax.all_gather(jnp.stack(blocks_of(0)), "dp", axis=0, tiled=False)
    later_own = jnp.stack(sum([blocks_of(layer) for layer in range(1, LAYERS)], []) + [prediction_matrix])
    later = lax.all_gather(jnp.stack([later_own, mv.y(later_own)]), "dp", axis=0, tiled=False)
    by_core = first_own.reshape((n_dp // 2, 2) + first_own.shape[1:])
    by_core = lax.dynamic_index_in_dim(by_core, me % 2, 1, keepdims=False)
    crossed = []

    def cross(pair, gate):
        send = by_core[:, 2 * pair : 2 * pair + 2]
        if pair >= 2:
            send = after(send, crossed[pair - 2])
        crossed.append(mv.y(send))
        got = crossed[-1] if gate is None else after(crossed[-1], gate)
        both = (got, mv.core(got))
        own = [[(first_own, 0, (2 * pair + index,))] * n_dp for index in range(2)]
        return [Matrix([own[index], [(array, 1, (index,)) for array in both for _ in range(n_dp // 2)]]) for index in range(2)]

    found = [Matrix([[(later, 0, (half, index))] * n_dp for half in range(2)]) for index in range(later_own.shape[0])]
    layers = [cross] + [found[6 * layer : 6 * layer + 6] for layer in range(LAYERS - 1)]
    head = found[-1]

    counts, pads = filled_sequence_segments[0], leading_filler_number[0]
    ends = jnp.cumsum(counts)
    starts = ends - counts
    first = starts + jnp.minimum(pads, counts - 1)
    cut = jnp.max(jnp.where(ends <= window, ends, 0))
    rows = jnp.where(second, skipped, 0) + jnp.arange(window, dtype=jnp.int32)
    begun = starts[None, :] <= rows[:, None]
    start_row = jnp.max(jnp.where(begun, starts[None, :], 0), axis=1)
    first_row = jnp.max(jnp.where(begun, first[None, :], 0), axis=1)
    real = rows >= first_row
    place = (rows - first_row).astype(F32)
    valid = jnp.where(second, rows >= cut, rows < cut)
    counted = real & valid
    allowed = (start_row[:, None] == start_row[None, :]) & (rows[None, :] <= rows[:, None])
    allowed = allowed & (real[None, :] | (rows[None, :] == rows[:, None]))
    bias = jnp.where(allowed, 0.0, NEG).astype(F32)
    is_first = (first_row[:, None] == rows[None, :]).astype(F32)

    half = HEAD // 2
    width = triple_projector_matrix.shape[3]
    freq = jnp.exp(-jnp.arange(half).astype(F32) * (2.0 * math.log(10000.0) / HEAD))
    angle = place[:, None] * freq[None, :]
    cosine, sine, none = jnp.cos(angle), jnp.sin(angle), jnp.zeros((window, half), F32)
    heads = width // HEAD
    tables = (
        jnp.tile(cosine, (1, 2 * heads)),
        jnp.tile(jnp.concatenate([-sine, none], axis=1), (1, heads)),
        jnp.tile(jnp.concatenate([none, sine], axis=1), (1, heads)),
    )

    points = mine(segment_matrix)
    firsts = jnp.dot(is_first, points, precision=HIGH)
    mean = jnp.mean(firsts, axis=1, keepdims=True)
    centred = firsts - mean
    spread = jnp.sqrt(jnp.mean(centred * centred, axis=1, keepdims=True))
    sigma = jnp.maximum(spread, FLOOR)
    scaled_low = jnp.where(real[:, None], (points - mean) / sigma, 0.0).astype(BF16)

    residual = jnp.einsum("tp,dp->td", scaled_low, embed, preferred_element_type=F32)
    saved = []
    for layer in range(LAYERS):
        residual, kept, layers[layer] = layer_forward(residual, layers[layer], gains[layer], bias, tables, order, width)
        saved.append(kept)

    as_column = lambda flags: flags[:, None].astype(F32)
    wide, flat, column = residual.shape, (window, width), (window, 1)
    rows_of = wide[1] // n_dp
    gain_grads = [[None, None] for _ in range(LAYERS)]
    scatter = Scatter(mv)
    early = []
    for layer in reversed(range(LAYERS)):
        wq, wk, wv, wo, wu, wd = layers[layer]
        mid, normed_ff, pre, hidden = saved[layer][7:]
        inner = (hidden, pre, normed_ff, mid, gains[layer][1:])
        if layer == LAYERS - 1:
            own, sent, mean_term, sigma_term, grad_res, gain_grads[layer][1], grads = run_kernel(
                head_body,
                (residual, mine(prediction_sensitivity), sens_other, as_column(real), as_column(counted), mean, sigma)
                + inner,
                (head, wd, wu),
                [(flat, F32), (flat, BF16), (column, F32), (column, F32), (wide, F32), ((1, wide[1]), F32)]
                + [((n_dp, 2, 3, rows_of, width), BF16)],
                order,
            )
            early.append(lax.psum_scatter(grads, "dp", scatter_dimension=0, tiled=False))
            proj, grads = attend_backward(grad_res, wo, saved[layer], tables, order, (n_dp, 2, 2, rows_of, width))
            early.append(lax.psum_scatter(grads, "dp", scatter_dimension=0, tiled=False))
            got = mv.y(sent)
            predictions = joined(own, got.astype(F32), cut)
            grad_res = after(grad_res, got)
        else:
            weight = ((2, wide[1] // 2, width), BF16)
            grad_res, gain_grads[layer][1], *grads = run_kernel(
                widen_back_body, (grad_res,) + inner, (wd, wu), [(wide, F32), ((1, wide[1]), F32)] + [weight] * 4, order
            )
            scatter.add(grads[:2], grads[2:])
            proj, *grads = attend_backward(after(grad_res, scatter.cores[-2]), wo, saved[layer], tables, order, None)
            scatter.add(grads[:2], grads[2:])
            proj = after(proj, scatter.second[-2])
        grad_res, gain_grads[layer][0], *grads = project_backward(
            grad_res, proj, layers[layer], gains[layer], saved[layer], order
        )
        scatter.add(grads[:2], grads[2:])
    grad_low = grad_res.astype(BF16)
    grad_scaled = jnp.einsum("td,dp->tp", grad_low, embed, preferred_element_type=F32)
    embed_term = jnp.einsum("td,tp->dp", grad_low, scaled_low, preferred_element_type=F32)

    grad_scaled = jnp.where(real[:, None], grad_scaled, 0.0)
    mean_row = mean_term - jnp.sum(grad_scaled, axis=1, keepdims=True) / sigma
    sigma_row = sigma_term - jnp.sum(grad_scaled * (points - mean), axis=1, keepdims=True) / (sigma * sigma)
    sums = lax.dot_general(
        is_first, jnp.concatenate([mean_row, sigma_row], axis=1), (((0,), (0,)), ((), ())), precision=HIGH
    )
    pull = jnp.where(spread > FLOOR, (points - mean) / jnp.maximum(spread, FLOOR), 0.0)
    patches = grad_scaled / sigma + sums[:, :1] / patch + sums[:, 1:] * pull / patch
    patches_grad = joined(patches, mv.y(patches), cut)

    tail = jnp.concatenate([embed_term] + [g.T for pair in gain_grads for g in pair], axis=1)
    n = tail.shape[0]
    tail = tail[: n // 2] + mv.core(tail[n // 2 :])
    tail = tail[: n // 4] + mv.x(tail[n // 4 :])
    tail = tail + mv.y(tail)
    n = tail.shape[0] // mv.q
    tail_out = tail[:n]
    for k in range(1, mv.q):
        tail_out = tail_out + mv.z(tail[k * n : (k + 1) * n], mv.q - k)
    w_in_grad = tail_out[:, :patch].T
    gains_grad = tail_out[:, patch:].T.reshape(LAYERS, 2, -1)

    scatter.finish()
    done = scatter.done
    early = jnp.concatenate(early, axis=1)
    early = early[0].astype(F32) + mv.y(early[1]).astype(F32)
    head_grad, down_last, up_last, attn_last, value_last = early
    qkv, attn = [[done[0][0], done[0][1], value_last]], [attn_last]
    up, down = [up_last], [down_last]
    at = 1
    for layer in reversed(range(LAYERS - 1)):
        down.append(done[at][0])
        up.append(done[at][1])
        attn.append(done[at + 1][0])
        qkv.append([done[at + 2][0], done[at + 2][1], done[at + 1][1]])
        at += 3
    return (
        predictions,
        patches_grad,
        w_in_grad,
        jnp.stack([jnp.stack(parts) for parts in qkv[::-1]]),
        jnp.stack([part.T for part in attn[::-1]]),
        jnp.stack(up[::-1]),
        jnp.stack([part.T for part in down[::-1]]),
        gains_grad,
        head_grad,
    )


def solution(mesh):
    placed = (
        P("dp", None),
        P("dp", None),
        P("dp", None),
        P(None, "dp"),
        P(None, None, "dp", "mp"),
        P(None, "mp", "dp"),
        P(None, "dp", "mp"),
        P(None, "mp", "dp"),
        P(None, None, "dp"),
        P("dp", "mp"),
        P("dp", "mp"),
    )
    return jax.shard_map(
        partial(on_device, n_dp=mesh.shape["dp"]),
        mesh=mesh,
        in_specs=placed,
        out_specs=(
            P("dp", "mp"),
            P("dp", None),
            P(None, "dp"),
            P(None, None, "dp", "mp"),
            P(None, "mp", "dp"),
            P(None, "dp", "mp"),
            P(None, "mp", "dp"),
            P(None, None, "dp"),
            P("dp", "mp"),
        ),
        check_vma=False,
    )
```

```python
from functools import partial
import math

import jax
import jax.numpy as jnp
from jax import lax
from jax.experimental import pallas as pl
from jax.experimental.pallas import tpu as pltpu
from jax.sharding import PartitionSpec as P

HEAD = 80
LAYERS = 2
MAXP = 64
EPS = 1e-06
FLOOR = 1.0
HIGH = lax.Precision.HIGHEST
NEG = -1e30
F32 = jnp.float32
BF16 = jnp.bfloat16
VMEM_LIMIT = 48 * 1024 * 1024
COST = int(1.15e11)


class Moves:
    def __init__(self, n_dp):
        self.q = n_dp // 4
        self.n = n_dp

    def core(self, v):
        return lax.ppermute(v, "dp", [(i, i ^ 1) for i in range(self.n)])

    def x(self, v):
        return lax.ppermute(v, "dp", [(i, i ^ 2) for i in range(self.n)])

    def z(self, v, k):
        return lax.ppermute(v, "dp", [(i, (i + 4 * k) % self.n) for i in range(self.n)])

    def y(self, v):
        return lax.ppermute(v, "mp", [(0, 1), (1, 0)])


def after(value, *earlier):
    return lax.optimization_barrier((value,) + earlier)[0]


def cat(parts, axis):
    return parts[0] if len(parts) == 1 else jnp.concatenate(parts, axis=axis)


def total(*parts):
    found = parts[0].astype(F32)
    for part in parts[1:]:
        found = found + part.astype(F32)
    return found


class Scatter:
    def __init__(self, mv):
        self.mv = mv
        self.history = []
        self.cores = []
        self.waiting = None
        self.last = None
        self.done = []
        self.second = []

    def step(self, to_x, to_y):
        if len(self.history) >= 2:
            to_x, to_y = after((to_x, to_y), self.history[-2])
        got = (self.mv.x(to_x), self.mv.y(to_y))
        self.history.append(got)
        return got

    def add(self, a, b):
        mv = self.mv
        (a_keep, a_send), (b_keep, b_send) = a, b
        a_got, b_got = mv.core(a_send), mv.core(b_send)
        self.cores.append(a_got)
        half = b_keep.shape[1] // 2
        to_y = total(a_keep[1], a_got[1]).astype(BF16)
        to_x = total(b_keep[:, half:], b_got[:, half:]).astype(BF16)
        from_x, from_y = self.step(to_x, to_y)
        self.second.append((from_x, from_y))
        if self.waiting is not None:
            self.finish()
        self.waiting = (a_keep[0], a_got[0], from_y), (b_keep[:, :half], b_got[:, :half], from_x)

    def finish(self):
        mv = self.mv
        a, b = self.waiting
        self.waiting = None
        half = a[0].shape[0] // 2
        to_x = total(*[part[half:] for part in a]).astype(BF16)
        from_x, from_y = self.step(to_x, total(*[part[1] for part in b]).astype(BF16))
        found = [total(*[part[:half] for part in a], from_x), total(*[part[0] for part in b], from_y)]
        rows = half // mv.q
        out = jnp.stack([part[:rows] for part in found])
        sends = [jnp.stack([part[k * rows : (k + 1) * rows].astype(BF16) for part in found]) for k in range(1, mv.q)]
        if self.last is not None:
            sends = after(sends, self.last)
        self.last = [mv.z(send, mv.q - k) for k, send in enumerate(sends, 1)]
        for got in self.last:
            out = out + got.astype(F32)
        self.done.append(out)


def dot(a, b, dims):
    return lax.dot_general(a, b, (dims, ((), ())), preferred_element_type=F32)


class Matrix:
    def __init__(self, halves):
        self.halves = halves
        self.rows, self.cols = halves[0][0][0].shape[-2:]

    def built(self, order):
        found = []
        for half in self.halves:
            blocks = []
            for place, (array, shift, index) in enumerate(half):
                block = lax.dynamic_index_in_dim(array, order[place] >> shift, 0, keepdims=False)
                blocks.append(block[index])
            found.append(jnp.concatenate(blocks))
        return jnp.stack(found)


def run_kernel(body, arrays, matrices, outs, order):
    sources, plan, shapes = [], [], []

    def source(array):
        for i, known in enumerate(sources):
            if known is array:
                return i
        sources.append(array)
        return len(sources) - 1

    for which, matrix in enumerate(matrices):
        if matrix.rows % 16:
            found = matrix.built(order)
            plan.append((which, None, source(found), None, None))
            shapes.append(found.shape)
            continue
        for half in range(2):
            for place, (array, shift, index) in enumerate(matrix.halves[half]):
                plan.append((which, (half, pl.ds(place * matrix.rows, matrix.rows)), source(array), (place, shift), index))
        shapes.append((2, len(matrix.halves[0]) * matrix.rows, matrix.cols))
    n_in, n_out = len(arrays), len(outs)
    n_all = n_in + 1 + len(sources)

    def kernel(*refs):
        inputs, order_ref, parts = refs[:n_in], refs[n_in], refs[n_in + 1 : n_all]
        outputs, scratch = refs[n_all : n_all + n_out], refs[n_all + n_out :]
        buffers, sems = scratch[:-1], scratch[-1]
        copies = [[] for _ in matrices]
        for number, (which, target, at, pick, index) in enumerate(plan):
            if target is None:
                copy = pltpu.make_async_copy(parts[at], buffers[which], sems.at[number])
            else:
                device = lax.shift_right_logical(order_ref[pick[0]], pick[1])
                copy = pltpu.make_async_copy(parts[at].at[(device,) + index], buffers[which].at[target], sems.at[number])
            copy.start()
            copies[which].append(copy)

        def weight(which):
            def ready():
                for copy in copies[which]:
                    copy.wait()
                return buffers[which]

            return ready

        body(inputs, [weight(which) for which in range(len(matrices))], outputs, order_ref)

    vmem = pl.BlockSpec(memory_space=pltpu.VMEM)
    return pl.pallas_call(
        kernel,
        in_specs=[vmem] * n_in
        + [pl.BlockSpec(memory_space=pltpu.SMEM)]
        + [pl.BlockSpec(memory_space=pl.ANY)] * len(sources),
        out_specs=[vmem] * n_out,
        out_shape=[jax.ShapeDtypeStruct(dims, kind) for dims, kind in outs],
        scratch_shapes=[pltpu.VMEM(dims, BF16) for dims in shapes] + [pltpu.SemaphoreType.DMA((max(1, len(plan)),))],
        compiler_params=pltpu.CompilerParams(vmem_limit_bytes=VMEM_LIMIT),
        cost_estimate=pl.CostEstimate(flops=COST, bytes_accessed=0, transcendentals=0),
    )(*arrays, order, *sources)


def head_windows(width):
    found = []
    for head in range(width // HEAD):
        low, high = head * HEAD, (head + 1) * HEAD
        found.append((low, high, low // 128 * 128, min(width, -(-high // 128) * 128)))
    return found


def in_head(low, high, start, stop):
    lane = lax.broadcasted_iota(jnp.int32, (1, stop - start), 1) + start
    return (lane >= low) & (lane < high)


def turn(values, cosine, ahead, behind):
    width = values.shape[-1]
    half = HEAD // 2
    return values * cosine + pltpu.roll(values, width - half, 1) * ahead + pltpu.roll(values, half, 1) * behind


def put(tiles, part, start, stop):
    for tile in range(start // 128, stop // 128):
        piece = part[:, tile * 128 - start : tile * 128 - start + 128]
        tiles[tile] = piece if tiles[tile] is None else tiles[tile] + piece


def gelu_parts(v):
    inner = math.sqrt(2.0 / math.pi) * (v + 0.044715 * (v * v * v))
    return jnp.tanh(inner)


def gelu_slope(v):
    tanh = gelu_parts(v)
    inner = math.sqrt(2.0 / math.pi) * (1.0 + 3.0 * 0.044715 * (v * v))
    return 0.5 * (1.0 + tanh) + 0.5 * v * (1.0 - tanh * tanh) * inner


def scale_of(values):
    return lax.rsqrt(jnp.mean(values * values, axis=-1, keepdims=True) + EPS)


def norm_back(values, gain, grad):
    scale = scale_of(values)
    plain = values * scale
    pushed = grad * gain
    back = scale * (pushed - plain * jnp.mean(pushed * plain, axis=-1, keepdims=True))
    return back, jnp.sum(grad * plain, axis=0, keepdims=True)


def split_grad(sink, half, values, grads):
    found = dot(values, grads, ((0,), (0,))).astype(BF16)
    if len(sink) == 2:
        keep, send = sink
        rows = keep.shape[1]
        keep[half] = found[:rows]
        send[half] = found[rows:]
    else:
        out, matrix, order = sink
        rows = out.shape[3]
        for place in range(out.shape[0]):
            out[order[place], half, matrix] = found[place * rows : (place + 1) * rows]


def project_body(inputs, weights, outputs, order):
    residual, gain, cosine, ahead, behind = inputs
    normed_out, q_out, k_out = outputs
    values = residual[...]
    normed = (values * scale_of(values) * gain[...]).astype(BF16)
    normed_out[...] = normed
    tables = (cosine[...], ahead[...], behind[...])
    for weight, out in zip(weights, (q_out, k_out)):
        matrix = weight()
        for half in range(2):
            out[half] = turn(dot(normed, matrix[half], ((1,), (0,))), *tables).astype(BF16)


def attend_body(inputs, weights, outputs, order):
    residual, normed, query, key, bias_ref = inputs
    mid_out, value_out, probs_out, attended_out = outputs
    width = query.shape[-1]
    scale = HEAD ** (-0.5)
    bias = bias_ref[...]
    matrix = weights[0]()
    for half in range(2):
        value_out[half] = dot(normed[...], matrix[half], ((1,), (0,))).astype(BF16)
    for half in range(2):
        tiles = [None] * (width // 128)
        for head, (low, high, start, stop) in enumerate(head_windows(width)):
            mine = in_head(low, high, start, stop)
            scores = dot(jnp.where(mine, query[half, :, start:stop], 0), key[half, :, start:stop], ((1,), (1,)))
            scores = scores * scale + bias
            grown = jnp.exp(scores - jnp.max(scores, axis=-1, keepdims=True))
            probs = (grown / jnp.sum(grown, axis=-1, keepdims=True)).astype(BF16)
            probs_out[half, head] = probs
            put(tiles, dot(probs, jnp.where(mine, value_out[half, :, start:stop], 0), ((1,), (0,))), start, stop)
        for tile, found in enumerate(tiles):
            attended_out[half, :, tile * 128 : tile * 128 + 128] = found.astype(BF16)
    matrix = weights[1]()
    mid = residual[...]
    for half in range(2):
        mid = mid + dot(attended_out[half], matrix[half], ((1,), (1,)))
    mid_out[...] = mid


def widen_body(inputs, weights, outputs, order):
    mid_ref, gain = inputs
    result_out, normed_out, pre_out, hidden_out = outputs
    mid = mid_ref[...]
    normed = (mid * scale_of(mid) * gain[...]).astype(BF16)
    normed_out[...] = normed
    matrix = weights[0]()
    for half in range(2):
        pre = dot(normed, matrix[half], ((1,), (0,)))
        pre_out[half] = pre
        hidden_out[half] = (0.5 * pre * (1.0 + gelu_parts(pre))).astype(BF16)
    matrix = weights[1]()
    for half in range(2):
        mid = mid + dot(hidden_out[half], matrix[half], ((1,), (1,)))
    result_out[...] = mid


def widen_back(grad, inputs, weights, outputs, down_sink, up_sink):
    hidden, pre, normed, mid, gain = inputs
    grad_out, gain_out = outputs
    low = grad.astype(BF16)
    down = weights[0]()
    back = None
    pushed = []
    for half in range(2):
        grad_hidden = dot(low, down[half], ((1,), (0,)))
        pushed.append((gelu_slope(pre[half]) * grad_hidden).astype(BF16))
        split_grad(down_sink, half, low, hidden[half])
    up = weights[1]()
    for half in range(2):
        split_grad(up_sink, half, normed[...], pushed[half])
        found = dot(pushed[half], up[half], ((1,), (1,)))
        back = found if back is None else back + found
    back, gain_out[...] = norm_back(mid[...], gain[...], back)
    grad_out[...] = grad + back


def head_body(inputs, weights, outputs, order):
    residual, sens_own, sens_other, real_ref, counted_ref, mean_ref, sigma_ref = inputs[:7]
    own_out, other_out, mean_out, sigma_out, grad_out, gain_out, weight_out = outputs
    final = residual[...].astype(BF16)
    real, counted = real_ref[...] > 0, counted_ref[...] > 0
    mean, sigma = mean_ref[...], sigma_ref[...]
    matrix = weights[0]()
    grad = mean_sum = sigma_sum = None
    sinks = [(weight_out, matrix, order) for matrix in range(3)]
    for half, (sens, out) in enumerate(((sens_own, own_out), (sens_other, other_out))):
        raw = dot(final, matrix[half], ((1,), (0,)))
        out[...] = jnp.where(real, raw * sigma + mean, 0.0).astype(out.dtype)
        cot = jnp.where(counted, sens[...].astype(F32), 0.0)
        graw = (cot * sigma).astype(BF16)
        split_grad(sinks[0], half, final, graw)
        back = dot(graw, matrix[half], ((1,), (1,)))
        parts = (back, jnp.sum(cot, axis=1, keepdims=True), jnp.sum(cot * raw, axis=1, keepdims=True))
        grad, mean_sum, sigma_sum = parts if half == 0 else (grad + parts[0], mean_sum + parts[1], sigma_sum + parts[2])
    mean_out[...] = mean_sum
    sigma_out[...] = sigma_sum
    widen_back(grad, inputs[7:], weights[1:], (grad_out, gain_out), sinks[1], sinks[2])


def widen_back_body(inputs, weights, outputs, order):
    grad_out, gain_out, *sinks = outputs
    widen_back(inputs[0][...], inputs[1:], weights, (grad_out, gain_out), sinks[:2], sinks[2:])


def attend_back_body(inputs, weights, outputs, order):
    grad_ref, attended, probs_ref, query_ref, key_ref, value_ref, normed, cosine, ahead, behind = inputs
    proj_out, *sinks = outputs
    if len(sinks) == 1:
        attn_sink, value_sink = (sinks[0], 0, order), (sinks[0], 1, order)
    else:
        attn_sink, value_sink = sinks[:2], sinks[2:]
    width = query_ref.shape[-1]
    scale = HEAD ** (-0.5)
    low = grad_ref[...].astype(BF16)
    matrix = weights[0]()
    tables = (cosine[...], -ahead[...], -behind[...])
    for half in range(2):
        grad_att = dot(low, matrix[half], ((1,), (0,))).astype(BF16)
        split_grad(attn_sink, half, low, attended[half])
        tiles = [[None] * (width // 128) for _ in range(3)]
        for head, (first, end, start, stop) in enumerate(head_windows(width)):
            mine = in_head(first, end, start, stop)
            grad = jnp.where(mine, grad_att[:, start:stop], 0)
            query = jnp.where(mine, query_ref[half, :, start:stop], 0)
            key = jnp.where(mine, key_ref[half, :, start:stop], 0)
            probs_low = probs_ref[half, head]
            probs = probs_low.astype(F32)
            grad_probs = dot(grad, value_ref[half, :, start:stop], ((1,), (1,)))
            delta = jnp.sum(grad_probs * probs, axis=-1, keepdims=True)
            grad_scores = (probs * (grad_probs - delta)).astype(BF16)
            put(tiles[0], dot(grad_scores, key, ((1,), (0,))), start, stop)
            put(tiles[1], dot(grad_scores, query, ((0,), (0,))), start, stop)
            put(tiles[2], dot(probs_low, grad, ((0,), (0,))), start, stop)
        for which in range(2):
            proj_out[which, half] = turn(jnp.concatenate(tiles[which], axis=1) * scale, *tables).astype(BF16)
        proj_out[2, half] = jnp.concatenate(tiles[2], axis=1).astype(BF16)
        split_grad(value_sink, half, normed[...], proj_out[2, half])


def project_back_body(inputs, weights, outputs, order):
    grad_ref, proj, normed, residual, gain = inputs
    grad_out, gain_out, *sinks = outputs
    for half in range(2):
        split_grad(sinks[:2], half, normed[...], proj[0, half])
        split_grad(sinks[2:], half, normed[...], proj[1, half])
    back = None
    for which in range(3):
        matrix = weights[which]()
        for half in range(2):
            found = dot(proj[which, half], matrix[half], ((1,), (1,)))
            back = found if back is None else back + found
    back, gain_out[...] = norm_back(residual[...], gain[...], back)
    grad_out[...] = grad_ref[...] + back


def layer_forward(residual, weights, gain, bias, tables, order, width):
    pairs = weights if callable(weights) else lambda pair, gate: weights[2 * pair : 2 * pair + 2]
    rows, features = residual.shape
    halves, wide = (2, rows, width), (rows, features)
    wq, wk = pairs(0, None)
    wv, wo = pairs(1, None)
    normed, q, k = run_kernel(
        project_body, (residual, gain[:1], *tables), (wq, wk), [(wide, BF16), (halves, BF16), (halves, BF16)], order
    )
    mid, v, probs, attended = run_kernel(
        attend_body,
        (residual, normed, q, k, bias),
        (wv, wo),
        [(wide, F32), (halves, BF16), ((2, width // HEAD, rows, rows), BF16), (halves, BF16)],
        order,
    )
    wu, wd = pairs(2, mid)
    result, normed_ff, pre, hidden = run_kernel(
        widen_body, (mid, gain[1:]), (wu, wd), [(wide, F32), (wide, BF16), (halves, F32), (halves, BF16)], order
    )
    return result, (residual, normed, q, k, v, probs, attended, mid, normed_ff, pre, hidden), (wq, wk, wv, wo, wu, wd)


def attend_backward(grad, wo, saved, tables, order, blocks):
    _, normed, q, k, v, probs, attended = saved[:7]
    features, (_, rows, width) = normed.shape[1], q.shape
    grads = [((2, features // 2, width), BF16)] * 4 if blocks is None else [(blocks, BF16)]
    return run_kernel(
        attend_back_body,
        (grad, attended, probs, q, k, v, normed, *tables),
        (wo,),
        [((3, 2, rows, width), BF16)] + grads,
        order,
    )


def project_backward(grad, proj, weights, gain, saved, order):
    residual, normed = saved[:2]
    rows, features = residual.shape
    weight = ((2, features // 2, proj.shape[-1]), BF16)
    return run_kernel(
        project_back_body,
        (grad, proj, normed, residual, gain[:1]),
        weights[:3],
        [((rows, features), F32), ((1, features), F32)] + [weight] * 4,
        order,
    )


def on_device(
    segment_matrix,
    filled_sequence_segments,
    leading_filler_number,
    segment_lifting_matrix,
    triple_projector_matrix,
    mixer_exit_matrix,
    widen_matrix,
    shrink_matrix,
    normalizer_factors,
    prediction_matrix,
    prediction_sensitivity,
    n_dp,
):
    mv = Moves(n_dp)
    tokens, patch = segment_matrix.shape
    window = tokens // 2 + MAXP // 2
    skipped = tokens - window
    second = lax.axis_index("mp") == 1

    def mine(values):
        return jnp.where(second, values[skipped:], values[:window])

    def other(values):
        return jnp.where(second, values[:window], values[skipped:])

    def joined(own, got, cut):
        front, back = jnp.where(second, got, own), jnp.where(second, own, got)
        rows = skipped + jnp.arange(window - skipped, dtype=jnp.int32)
        shared = jnp.where((rows < cut)[:, None], front[skipped:], back[: window - skipped])
        return jnp.concatenate([front[:skipped], shared, back[window - skipped :]])

    small = jnp.concatenate(
        [segment_lifting_matrix.T, normalizer_factors.reshape(2 * LAYERS, -1).T], axis=1
    )
    small = cat([small] + [mv.z(small, k) for k in range(1, mv.q)], 0)
    small = jnp.concatenate([small, mv.x(small)])
    small = jnp.concatenate([small, mv.core(small)])
    embed = small[:, :patch]
    gains = small[:, patch:].T.astype(F32).reshape(LAYERS, 2, -1)
    sens_other = mv.y(other(prediction_sensitivity))

    def blocks_of(layer):
        qkv = [triple_projector_matrix[layer, c] for c in range(3)]
        return qkv + [mixer_exit_matrix[layer].T, widen_matrix[layer], shrink_matrix[layer].T]

    me = lax.axis_index("dp")
    place = jnp.arange(n_dp, dtype=jnp.int32)
    bits, behind = place // mv.q, place % mv.q
    order = ((me // 4 - behind) % mv.q * 4 + me % 4) ^ (2 * (bits % 2)) ^ (bits // 2)

    first_own = lax.all_gather(jnp.stack(blocks_of(0)), "dp", axis=0, tiled=False)
    later_own = jnp.stack(sum([blocks_of(layer) for layer in range(1, LAYERS)], []) + [prediction_matrix])
    later = lax.all_gather(jnp.stack([later_own, mv.y(later_own)]), "dp", axis=0, tiled=False)
    by_core = first_own.reshape((n_dp // 2, 2) + first_own.shape[1:])
    by_core = lax.dynamic_index_in_dim(by_core, me % 2, 1, keepdims=False)
    crossed = []

    def cross(pair, gate):
        send = by_core[:, 2 * pair : 2 * pair + 2]
        if pair >= 2:
            send = after(send, crossed[pair - 2])
        crossed.append(mv.y(send))
        got = crossed[-1] if gate is None else after(crossed[-1], gate)
        both = (got, mv.core(got))
        own = [[(first_own, 0, (2 * pair + index,))] * n_dp for index in range(2)]
        return [Matrix([own[index], [(array, 1, (index,)) for array in both for _ in range(n_dp // 2)]]) for index in range(2)]

    found = [Matrix([[(later, 0, (half, index))] * n_dp for half in range(2)]) for index in range(later_own.shape[0])]
    layers = [cross] + [found[6 * layer : 6 * layer + 6] for layer in range(LAYERS - 1)]
    head = found[-1]

    counts, pads = filled_sequence_segments[0], leading_filler_number[0]
    ends = jnp.cumsum(counts)
    starts = ends - counts
    first = starts + jnp.minimum(pads, counts - 1)
    cut = jnp.max(jnp.where(ends <= window, ends, 0))
    rows = jnp.where(second, skipped, 0) + jnp.arange(window, dtype=jnp.int32)
    begun = starts[None, :] <= rows[:, None]
    start_row = jnp.max(jnp.where(begun, starts[None, :], 0), axis=1)
    first_row = jnp.max(jnp.where(begun, first[None, :], 0), axis=1)
    real = rows >= first_row
    place = (rows - first_row).astype(F32)
    valid = jnp.where(second, rows >= cut, rows < cut)
    counted = real & valid
    allowed = (start_row[:, None] == start_row[None, :]) & (rows[None, :] <= rows[:, None])
    allowed = allowed & (real[None, :] | (rows[None, :] == rows[:, None]))
    bias = jnp.where(allowed, 0.0, NEG).astype(F32)
    is_first = (first_row[:, None] == rows[None, :]).astype(F32)

    half = HEAD // 2
    width = triple_projector_matrix.shape[3]
    freq = jnp.exp(-jnp.arange(half).astype(F32) * (2.0 * math.log(10000.0) / HEAD))
    angle = place[:, None] * freq[None, :]
    cosine, sine, none = jnp.cos(angle), jnp.sin(angle), jnp.zeros((window, half), F32)
    heads = width // HEAD
    tables = (
        jnp.tile(cosine, (1, 2 * heads)),
        jnp.tile(jnp.concatenate([-sine, none], axis=1), (1, heads)),
        jnp.tile(jnp.concatenate([none, sine], axis=1), (1, heads)),
    )

    points = mine(segment_matrix)
    firsts = jnp.dot(is_first, points, precision=HIGH)
    mean = jnp.mean(firsts, axis=1, keepdims=True)
    centred = firsts - mean
    spread = jnp.sqrt(jnp.mean(centred * centred, axis=1, keepdims=True))
    sigma = jnp.maximum(spread, FLOOR)
    scaled_low = jnp.where(real[:, None], (points - mean) / sigma, 0.0).astype(BF16)

    residual = jnp.einsum("tp,dp->td", scaled_low, embed, preferred_element_type=F32)
    saved = []
    for layer in range(LAYERS):
        residual, kept, layers[layer] = layer_forward(residual, layers[layer], gains[layer], bias, tables, order, width)
        saved.append(kept)

    as_column = lambda flags: flags[:, None].astype(F32)
    wide, flat, column = residual.shape, (window, width), (window, 1)
    rows_of = wide[1] // n_dp
    gain_grads = [[None, None] for _ in range(LAYERS)]
    scatter = Scatter(mv)
    early = []
    for layer in reversed(range(LAYERS)):
        wq, wk, wv, wo, wu, wd = layers[layer]
        mid, normed_ff, pre, hidden = saved[layer][7:]
        inner = (hidden, pre, normed_ff, mid, gains[layer][1:])
        if layer == LAYERS - 1:
            own, sent, mean_term, sigma_term, grad_res, gain_grads[layer][1], grads = run_kernel(
                head_body,
                (residual, mine(prediction_sensitivity), sens_other, as_column(real), as_column(counted), mean, sigma)
                + inner,
                (head, wd, wu),
                [(flat, F32), (flat, BF16), (column, F32), (column, F32), (wide, F32), ((1, wide[1]), F32)]
                + [((n_dp, 2, 3, rows_of, width), BF16)],
                order,
            )
            early.append(lax.psum_scatter(grads, "dp", scatter_dimension=0, tiled=True))
            got = mv.y(sent)
            predictions = joined(own, got.astype(F32), cut)
            proj, grads = attend_backward(grad_res, wo, saved[layer], tables, order, (n_dp, 2, 2, rows_of, width))
            early.append(lax.psum_scatter(grads, "dp", scatter_dimension=0, tiled=True))
            grad_res = after(grad_res, got)
        else:
            weight = ((2, wide[1] // 2, width), BF16)
            grad_res, gain_grads[layer][1], *grads = run_kernel(
                widen_back_body, (grad_res,) + inner, (wd, wu), [(wide, F32), ((1, wide[1]), F32)] + [weight] * 4, order
            )
            scatter.add(grads[:2], grads[2:])
            grad_res = after(grad_res, scatter.cores[-2])
            proj, *grads = attend_backward(grad_res, wo, saved[layer], tables, order, None)
            scatter.add(grads[:2], grads[2:])
            proj = after(proj, scatter.second[-2])
        grad_res, gain_grads[layer][0], *grads = project_backward(
            grad_res, proj, layers[layer], gains[layer], saved[layer], order
        )
        scatter.add(grads[:2], grads[2:])
    grad_low = grad_res.astype(BF16)
    grad_scaled = jnp.einsum("td,dp->tp", grad_low, embed, preferred_element_type=F32)
    embed_term = jnp.einsum("td,tp->dp", grad_low, scaled_low, preferred_element_type=F32)

    grad_scaled = jnp.where(real[:, None], grad_scaled, 0.0)
    mean_row = mean_term - jnp.sum(grad_scaled, axis=1, keepdims=True) / sigma
    sigma_row = sigma_term - jnp.sum(grad_scaled * (points - mean), axis=1, keepdims=True) / (sigma * sigma)
    sums = lax.dot_general(
        is_first, jnp.concatenate([mean_row, sigma_row], axis=1), (((0,), (0,)), ((), ())), precision=HIGH
    )
    pull = jnp.where(spread > FLOOR, (points - mean) / jnp.maximum(spread, FLOOR), 0.0)
    patches = grad_scaled / sigma + sums[:, :1] / patch + sums[:, 1:] * pull / patch
    patches_grad = joined(patches, mv.y(patches), cut)

    tail = jnp.concatenate([embed_term] + [g.T for pair in gain_grads for g in pair], axis=1)
    n = tail.shape[0]
    tail = tail[: n // 2] + mv.core(tail[n // 2 :])
    tail = tail[: n // 4] + mv.x(tail[n // 4 :])
    tail = tail + mv.y(tail)
    n = tail.shape[0] // mv.q
    tail_out = tail[:n]
    for k in range(1, mv.q):
        tail_out = tail_out + mv.z(tail[k * n : (k + 1) * n], mv.q - k)
    w_in_grad = tail_out[:, :patch].T
    gains_grad = tail_out[:, patch:].T.reshape(LAYERS, 2, -1)

    scatter.finish()
    done = iter(scatter.done)
    early = jnp.concatenate([part[0] for part in early], axis=1)
    early = early[0].astype(F32) + mv.y(early[1]).astype(F32)
    head_grad, down_last, up_last, attn_last, value_last = early
    query_part, key_part = next(done)
    qkv, attn = [[query_part, key_part, value_last]], [attn_last]
    up, down = [up_last], [down_last]
    for layer in reversed(range(LAYERS - 1)):
        pair = next(done)
        down.append(pair[0])
        up.append(pair[1])
        attn_part, value_part = next(done)
        query_part, key_part = next(done)
        attn.append(attn_part)
        qkv.append([query_part, key_part, value_part])
    return (
        predictions,
        patches_grad,
        w_in_grad,
        jnp.stack([jnp.stack(parts) for parts in qkv[::-1]]),
        jnp.stack([part.T for part in attn[::-1]]),
        jnp.stack(up[::-1]),
        jnp.stack([part.T for part in down[::-1]]),
        gains_grad,
        head_grad,
    )


def solution(mesh):
    placed = (
        P("dp", None),
        P("dp", None),
        P("dp", None),
        P(None, "dp"),
        P(None, None, "dp", "mp"),
        P(None, "mp", "dp"),
        P(None, "dp", "mp"),
        P(None, "mp", "dp"),
        P(None, None, "dp"),
        P("dp", "mp"),
        P("dp", "mp"),
    )
    return jax.shard_map(
        partial(on_device, n_dp=mesh.shape["dp"]),
        mesh=mesh,
        in_specs=placed,
        out_specs=(
            P("dp", "mp"),
            P("dp", None),
            P(None, "dp"),
            P(None, None, "dp", "mp"),
            P(None, "mp", "dp"),
            P(None, "dp", "mp"),
            P(None, "mp", "dp"),
            P(None, None, "dp"),
            P("dp", "mp"),
        ),
        check_vma=False,
    )
```

```python
from functools import partial
import math

import jax
import jax.numpy as jnp
from jax import lax
from jax.experimental import pallas as pl
from jax.experimental.pallas import tpu as pltpu
from jax.sharding import PartitionSpec as P

HEAD = 80
LAYERS = 2
MAXP = 64
EPS = 1e-06
FLOOR = 1.0
HIGH = lax.Precision.HIGHEST
NEG = -1e30
F32 = jnp.float32
BF16 = jnp.bfloat16
VMEM_LIMIT = 48 * 1024 * 1024
COST = int(1.15e11)


class Moves:
    def __init__(self, n_dp):
        self.q = n_dp // 4
        self.n = n_dp

    def core(self, v):
        return lax.ppermute(v, "dp", [(i, i ^ 1) for i in range(self.n)])

    def x(self, v):
        return lax.ppermute(v, "dp", [(i, i ^ 2) for i in range(self.n)])

    def z(self, v, k):
        return lax.ppermute(v, "dp", [(i, (i + 4 * k) % self.n) for i in range(self.n)])

    def y(self, v):
        return lax.ppermute(v, "mp", [(0, 1), (1, 0)])


def after(value, *earlier):
    return lax.optimization_barrier((value,) + earlier)[0]


def cat(parts, axis):
    return parts[0] if len(parts) == 1 else jnp.concatenate(parts, axis=axis)


def total(*parts):
    found = parts[0].astype(F32)
    for part in parts[1:]:
        found = found + part.astype(F32)
    return found


class Scatter:
    def __init__(self, mv):
        self.mv = mv
        self.history = []
        self.cores = []
        self.waiting = None
        self.last = None
        self.done = []
        self.second = []

    def step(self, to_x, to_y):
        if len(self.history) >= 2:
            if to_x is None:
                to_y = after(to_y, self.history[-2])
            else:
                to_x, to_y = after((to_x, to_y), self.history[-2])
        got = (None if to_x is None else self.mv.x(to_x), self.mv.y(to_y))
        self.history.append(got)
        return got

    def add(self, a, b):
        mv = self.mv
        a_keep, a_send = a
        a_got = mv.core(a_send)
        self.cores.append(a_got)
        to_y = total(a_keep[1], a_got[1]).astype(BF16)
        if b is None:
            _, from_y = self.step(None, to_y)
            self.second.append(from_y)
            entry = ((a_keep[0], a_got[0], from_y), None)
        else:
            b_keep, b_send = b
            b_got = mv.core(b_send)
            half = b_keep.shape[1] // 2
            to_x = total(b_keep[:, half:], b_got[:, half:]).astype(BF16)
            from_x, from_y = self.step(to_x, to_y)
            self.second.append((from_x, from_y))
            entry = ((a_keep[0], a_got[0], from_y), (b_keep[:, :half], b_got[:, :half], from_x))
        if self.waiting is not None:
            self.finish()
        self.waiting = entry

    def finish(self):
        mv = self.mv
        a, b = self.waiting
        self.waiting = None
        half = a[0].shape[0] // 2
        to_x = total(*[part[half:] for part in a]).astype(BF16)
        if b is None:
            from_x = mv.x(to_x)
            found = [total(*[part[:half] for part in a], from_x)]
        else:
            from_x, from_y = self.step(to_x, total(*[part[1] for part in b]).astype(BF16))
            found = [total(*[part[:half] for part in a], from_x), total(*[part[0] for part in b], from_y)]
        rows = half // mv.q
        out = jnp.stack([part[:rows] for part in found])
        sends = [jnp.stack([part[k * rows : (k + 1) * rows].astype(BF16) for part in found]) for k in range(1, mv.q)]
        if self.last is not None:
            sends = after(sends, self.last)
        self.last = [mv.z(send, mv.q - k) for k, send in enumerate(sends, 1)]
        for got in self.last:
            out = out + got.astype(F32)
        self.done.append(out)


def dot(a, b, dims):
    return lax.dot_general(a, b, (dims, ((), ())), preferred_element_type=F32)


class Matrix:
    def __init__(self, halves):
        self.halves = halves
        self.rows, self.cols = halves[0][0][0].shape[-2:]

    def built(self, order):
        found = []
        for half in self.halves:
            blocks = []
            for place, (array, shift, index) in enumerate(half):
                block = lax.dynamic_index_in_dim(array, order[place] >> shift, 0, keepdims=False)
                blocks.append(block[index])
            found.append(jnp.concatenate(blocks))
        return jnp.stack(found)


def run_kernel(body, arrays, matrices, outs, order, earlier=None):
    sources, plan, shapes = [], [], []

    def source(array):
        for i, known in enumerate(sources):
            if known is array:
                return i
        sources.append(array)
        return len(sources) - 1

    for which, matrix in enumerate(matrices):
        if matrix.rows % 16:
            found = matrix.built(order)
            plan.append((which, None, source(found), None, None))
            shapes.append(found.shape)
            continue
        for half in range(2):
            for place, (array, shift, index) in enumerate(matrix.halves[half]):
                plan.append((which, (half, pl.ds(place * matrix.rows, matrix.rows)), source(array), (place, shift), index))
        shapes.append((2, len(matrix.halves[0]) * matrix.rows, matrix.cols))
    n_in, n_out = len(arrays), len(outs)
    if earlier is not None:
        source(earlier)
        part = outs[-1][0]
        count = earlier.shape[2]
        outs = outs[:-1] + [(part[:2] + (count + part[2],) + part[3:], BF16)]
    n_all = n_in + 1 + len(sources)

    def kernel(*refs):
        inputs, order_ref, parts = refs[:n_in], refs[n_in], refs[n_in + 1 : n_all]
        outputs, scratch = refs[n_all : n_all + n_out], refs[n_all + n_out :]
        if earlier is not None:
            join_sem, scratch = scratch[-1], scratch[:-1]
            join = pltpu.make_async_copy(parts[-1], outputs[-1].at[:, :, pl.ds(0, count)], join_sem.at[0])
        buffers, sems = scratch[:-1], scratch[-1]
        copies = [[] for _ in matrices]
        for number, (which, target, at, pick, index) in enumerate(plan):
            if target is None:
                copy = pltpu.make_async_copy(parts[at], buffers[which], sems.at[number])
            else:
                device = lax.shift_right_logical(order_ref[pick[0]], pick[1])
                copy = pltpu.make_async_copy(parts[at].at[(device,) + index], buffers[which].at[target], sems.at[number])
            copy.start()
            copies[which].append(copy)

        def weight(which):
            def ready():
                for copy in copies[which]:
                    copy.wait()
                return buffers[which]

            return ready

        if earlier is not None:
            join.start()
        body(inputs, [weight(which) for which in range(len(matrices))], outputs, order_ref)
        if earlier is not None:
            join.wait()

    vmem = pl.BlockSpec(memory_space=pltpu.VMEM)
    return pl.pallas_call(
        kernel,
        in_specs=[vmem] * n_in
        + [pl.BlockSpec(memory_space=pltpu.SMEM)]
        + [pl.BlockSpec(memory_space=pl.ANY)] * len(sources),
        out_specs=[vmem] * n_out,
        out_shape=[jax.ShapeDtypeStruct(dims, kind) for dims, kind in outs],
        scratch_shapes=[pltpu.VMEM(dims, BF16) for dims in shapes]
        + [pltpu.SemaphoreType.DMA((max(1, len(plan)),))]
        + ([] if earlier is None else [pltpu.SemaphoreType.DMA((1,))]),
        compiler_params=pltpu.CompilerParams(vmem_limit_bytes=VMEM_LIMIT),
        cost_estimate=pl.CostEstimate(flops=COST, bytes_accessed=0, transcendentals=0),
    )(*arrays, order, *sources)


def head_windows(width):
    found = []
    for head in range(width // HEAD):
        low, high = head * HEAD, (head + 1) * HEAD
        found.append((low, high, low // 128 * 128, min(width, -(-high // 128) * 128)))
    return found


def in_head(low, high, start, stop):
    lane = lax.broadcasted_iota(jnp.int32, (1, stop - start), 1) + start
    return (lane >= low) & (lane < high)


def turn(values, cosine, ahead, behind):
    width = values.shape[-1]
    half = HEAD // 2
    return values * cosine + pltpu.roll(values, width - half, 1) * ahead + pltpu.roll(values, half, 1) * behind


def put(tiles, part, start, stop):
    for tile in range(start // 128, stop // 128):
        piece = part[:, tile * 128 - start : tile * 128 - start + 128]
        tiles[tile] = piece if tiles[tile] is None else tiles[tile] + piece


def gelu_parts(v):
    inner = math.sqrt(2.0 / math.pi) * (v + 0.044715 * (v * v * v))
    return jnp.tanh(inner)


def gelu_slope(v):
    tanh = gelu_parts(v)
    inner = math.sqrt(2.0 / math.pi) * (1.0 + 3.0 * 0.044715 * (v * v))
    return 0.5 * (1.0 + tanh) + 0.5 * v * (1.0 - tanh * tanh) * inner


def scale_of(values):
    return lax.rsqrt(jnp.mean(values * values, axis=-1, keepdims=True) + EPS)


def norm_back(values, gain, grad):
    scale = scale_of(values)
    plain = values * scale
    pushed = grad * gain
    back = scale * (pushed - plain * jnp.mean(pushed * plain, axis=-1, keepdims=True))
    return back, jnp.sum(grad * plain, axis=0, keepdims=True)


def split_grad(sink, half, values, grads):
    found = dot(values, grads, ((0,), (0,))).astype(BF16)
    if len(sink) == 2:
        keep, send = sink
        rows = keep.shape[1]
        keep[half] = found[:rows]
        send[half] = found[rows:]
    else:
        out, matrix, order = sink
        rows = out.shape[3]
        for place in range(out.shape[0]):
            out[order[place], half, matrix] = found[place * rows : (place + 1) * rows]


def project_body(inputs, weights, outputs, order):
    residual, gain, cosine, ahead, behind = inputs
    normed_out, q_out, k_out = outputs
    values = residual[...]
    normed = (values * scale_of(values) * gain[...]).astype(BF16)
    normed_out[...] = normed
    tables = (cosine[...], ahead[...], behind[...])
    for weight, out in zip(weights, (q_out, k_out)):
        matrix = weight()
        for half in range(2):
            out[half] = turn(dot(normed, matrix[half], ((1,), (0,))), *tables).astype(BF16)


def attend_body(inputs, weights, outputs, order):
    residual, normed, query, key, bias_ref = inputs
    mid_out, value_out, probs_out, attended_out = outputs
    width = query.shape[-1]
    scale = HEAD ** (-0.5)
    bias = bias_ref[...]
    matrix = weights[0]()
    for half in range(2):
        value_out[half] = dot(normed[...], matrix[half], ((1,), (0,))).astype(BF16)
    for half in range(2):
        tiles = [None] * (width // 128)
        for head, (low, high, start, stop) in enumerate(head_windows(width)):
            mine = in_head(low, high, start, stop)
            scores = dot(jnp.where(mine, query[half, :, start:stop], 0), key[half, :, start:stop], ((1,), (1,)))
            scores = scores * scale + bias
            grown = jnp.exp(scores - jnp.max(scores, axis=-1, keepdims=True))
            probs = (grown / jnp.sum(grown, axis=-1, keepdims=True)).astype(BF16)
            probs_out[half, head] = probs
            put(tiles, dot(probs, jnp.where(mine, value_out[half, :, start:stop], 0), ((1,), (0,))), start, stop)
        for tile, found in enumerate(tiles):
            attended_out[half, :, tile * 128 : tile * 128 + 128] = found.astype(BF16)
    matrix = weights[1]()
    mid = residual[...]
    for half in range(2):
        mid = mid + dot(attended_out[half], matrix[half], ((1,), (1,)))
    mid_out[...] = mid


def widen_body(inputs, weights, outputs, order):
    mid_ref, gain = inputs
    result_out, normed_out, pre_out, hidden_out = outputs
    mid = mid_ref[...]
    normed = (mid * scale_of(mid) * gain[...]).astype(BF16)
    normed_out[...] = normed
    matrix = weights[0]()
    for half in range(2):
        pre = dot(normed, matrix[half], ((1,), (0,)))
        pre_out[half] = pre
        hidden_out[half] = (0.5 * pre * (1.0 + gelu_parts(pre))).astype(BF16)
    matrix = weights[1]()
    for half in range(2):
        mid = mid + dot(hidden_out[half], matrix[half], ((1,), (1,)))
    result_out[...] = mid


def widen_back(grad, inputs, weights, outputs, down_sink, up_sink):
    hidden, pre, normed, mid, gain = inputs
    grad_out, gain_out = outputs
    low = grad.astype(BF16)
    down = weights[0]()
    back = None
    pushed = []
    for half in range(2):
        grad_hidden = dot(low, down[half], ((1,), (0,)))
        pushed.append((gelu_slope(pre[half]) * grad_hidden).astype(BF16))
        split_grad(down_sink, half, low, hidden[half])
    up = weights[1]()
    for half in range(2):
        split_grad(up_sink, half, normed[...], pushed[half])
        found = dot(pushed[half], up[half], ((1,), (1,)))
        back = found if back is None else back + found
    back, gain_out[...] = norm_back(mid[...], gain[...], back)
    grad_out[...] = grad + back


def head_body(inputs, weights, outputs, order):
    residual, sens_own, sens_other, real_ref, counted_ref, mean_ref, sigma_ref = inputs[:7]
    own_out, other_out, mean_out, sigma_out, grad_out, gain_out, weight_out = outputs
    final = residual[...].astype(BF16)
    real, counted = real_ref[...] > 0, counted_ref[...] > 0
    mean, sigma = mean_ref[...], sigma_ref[...]
    matrix = weights[0]()
    grad = mean_sum = sigma_sum = None
    for half, (sens, out) in enumerate(((sens_own, own_out), (sens_other, other_out))):
        raw = dot(final, matrix[half], ((1,), (0,)))
        out[...] = jnp.where(real, raw * sigma + mean, 0.0).astype(out.dtype)
        cot = jnp.where(counted, sens[...].astype(F32), 0.0)
        graw = (cot * sigma).astype(BF16)
        split_grad((weight_out, 0, order), half, final, graw)
        back = dot(graw, matrix[half], ((1,), (1,)))
        parts = (back, jnp.sum(cot, axis=1, keepdims=True), jnp.sum(cot * raw, axis=1, keepdims=True))
        grad, mean_sum, sigma_sum = parts if half == 0 else (grad + parts[0], mean_sum + parts[1], sigma_sum + parts[2])
    mean_out[...] = mean_sum
    sigma_out[...] = sigma_sum
    widen_back(grad, inputs[7:], weights[1:], (grad_out, gain_out), (weight_out, 1, order), (weight_out, 2, order))


def widen_back_body(inputs, weights, outputs, order):
    grad_out, gain_out, *sinks = outputs
    widen_back(inputs[0][...], inputs[1:], weights, (grad_out, gain_out), sinks[:2], sinks[2:])


def attend_back_body(inputs, weights, outputs, order):
    grad_ref, attended, probs_ref, query_ref, key_ref, value_ref, normed, cosine, ahead, behind = inputs
    proj_out, *sinks = outputs
    if len(sinks) == 1:
        at = sinks[0].shape[2] - 2
        attn_sink, value_sink = (sinks[0], at, order), (sinks[0], at + 1, order)
    else:
        attn_sink, value_sink = sinks[:2], sinks[2:]
    width = query_ref.shape[-1]
    scale = HEAD ** (-0.5)
    low = grad_ref[...].astype(BF16)
    matrix = weights[0]()
    tables = (cosine[...], -ahead[...], -behind[...])
    for half in range(2):
        grad_att = dot(low, matrix[half], ((1,), (0,))).astype(BF16)
        split_grad(attn_sink, half, low, attended[half])
        tiles = [[None] * (width // 128) for _ in range(3)]
        for head, (first, end, start, stop) in enumerate(head_windows(width)):
            mine = in_head(first, end, start, stop)
            grad = jnp.where(mine, grad_att[:, start:stop], 0)
            query = jnp.where(mine, query_ref[half, :, start:stop], 0)
            key = jnp.where(mine, key_ref[half, :, start:stop], 0)
            probs_low = probs_ref[half, head]
            probs = probs_low.astype(F32)
            grad_probs = dot(grad, value_ref[half, :, start:stop], ((1,), (1,)))
            delta = jnp.sum(grad_probs * probs, axis=-1, keepdims=True)
            grad_scores = (probs * (grad_probs - delta)).astype(BF16)
            put(tiles[0], dot(grad_scores, key, ((1,), (0,))), start, stop)
            put(tiles[1], dot(grad_scores, query, ((0,), (0,))), start, stop)
            put(tiles[2], dot(probs_low, grad, ((0,), (0,))), start, stop)
        for which in range(2):
            proj_out[which, half] = turn(jnp.concatenate(tiles[which], axis=1) * scale, *tables).astype(BF16)
        proj_out[2, half] = jnp.concatenate(tiles[2], axis=1).astype(BF16)
        split_grad(value_sink, half, normed[...], proj_out[2, half])


def project_back_body(inputs, weights, outputs, order):
    grad_ref, proj, normed, residual, gain = inputs
    grad_out, gain_out, *sinks = outputs
    for half in range(2):
        split_grad(sinks[:2], half, normed[...], proj[0, half])
        split_grad(sinks[2:], half, normed[...], proj[1, half])
    back = None
    for which in range(3):
        matrix = weights[which]()
        for half in range(2):
            found = dot(proj[which, half], matrix[half], ((1,), (1,)))
            back = found if back is None else back + found
    back, gain_out[...] = norm_back(residual[...], gain[...], back)
    grad_out[...] = grad_ref[...] + back


def layer_forward(residual, weights, gain, bias, tables, order, width):
    pairs = weights if callable(weights) else lambda pair, gate: weights[2 * pair : 2 * pair + 2]
    rows, features = residual.shape
    halves, wide = (2, rows, width), (rows, features)
    wq, wk = pairs(0, None)
    wv, wo = pairs(1, None)
    normed, q, k = run_kernel(
        project_body, (residual, gain[:1], *tables), (wq, wk), [(wide, BF16), (halves, BF16), (halves, BF16)], order
    )
    mid, v, probs, attended = run_kernel(
        attend_body,
        (residual, normed, q, k, bias),
        (wv, wo),
        [(wide, F32), (halves, BF16), ((2, width // HEAD, rows, rows), BF16), (halves, BF16)],
        order,
    )
    wu, wd = pairs(2, mid)
    result, normed_ff, pre, hidden = run_kernel(
        widen_body, (mid, gain[1:]), (wu, wd), [(wide, F32), (wide, BF16), (halves, F32), (halves, BF16)], order
    )
    return result, (residual, normed, q, k, v, probs, attended, mid, normed_ff, pre, hidden), (wq, wk, wv, wo, wu, wd)


def attend_backward(grad, wo, saved, tables, order, earlier=None):
    _, normed, q, k, v, probs, attended = saved[:7]
    features, (_, rows, width) = normed.shape[1], q.shape
    if earlier is None:
        grads = [((2, features // 2, width), BF16)] * 4
    else:
        grads = [(earlier.shape[:2] + (2,) + earlier.shape[3:], BF16)]
    return run_kernel(
        attend_back_body,
        (grad, attended, probs, q, k, v, normed, *tables),
        (wo,),
        [((3, 2, rows, width), BF16)] + grads,
        order,
        earlier,
    )


def project_backward(grad, proj, weights, gain, saved, order):
    residual, normed = saved[:2]
    rows, features = residual.shape
    weight = ((2, features // 2, proj.shape[-1]), BF16)
    return run_kernel(
        project_back_body,
        (grad, proj, normed, residual, gain[:1]),
        weights[:3],
        [((rows, features), F32), ((1, features), F32)] + [weight] * 4,
        order,
    )


def on_device(
    segment_matrix,
    filled_sequence_segments,
    leading_filler_number,
    segment_lifting_matrix,
    triple_projector_matrix,
    mixer_exit_matrix,
    widen_matrix,
    shrink_matrix,
    normalizer_factors,
    prediction_matrix,
    prediction_sensitivity,
    n_dp,
):
    mv = Moves(n_dp)
    tokens, patch = segment_matrix.shape
    window = tokens // 2 + MAXP // 2
    skipped = tokens - window
    second = lax.axis_index("mp") == 1

    def mine(values):
        return jnp.where(second, values[skipped:], values[:window])

    def other(values):
        return jnp.where(second, values[:window], values[skipped:])

    def joined(own, got, cut):
        front, back = jnp.where(second, got, own), jnp.where(second, own, got)
        rows = skipped + jnp.arange(window - skipped, dtype=jnp.int32)
        shared = jnp.where((rows < cut)[:, None], front[skipped:], back[: window - skipped])
        return jnp.concatenate([front[:skipped], shared, back[window - skipped :]])

    small = jnp.concatenate(
        [segment_lifting_matrix.T, normalizer_factors.reshape(2 * LAYERS, -1).T], axis=1
    )
    small = cat([small] + [mv.z(small, k) for k in range(1, mv.q)], 0)
    small = jnp.concatenate([small, mv.x(small)])
    small = jnp.concatenate([small, mv.core(small)])
    embed = small[:, :patch]
    gains = small[:, patch:].T.astype(F32).reshape(LAYERS, 2, -1)
    sens_other = mv.y(other(prediction_sensitivity))

    def blocks_of(layer):
        qkv = [triple_projector_matrix[layer, c] for c in range(3)]
        return qkv + [mixer_exit_matrix[layer].T, widen_matrix[layer], shrink_matrix[layer].T]

    me = lax.axis_index("dp")
    place = jnp.arange(n_dp, dtype=jnp.int32)
    bits, behind = place // mv.q, place % mv.q
    order = ((me // 4 - behind) % mv.q * 4 + me % 4) ^ (2 * (bits % 2)) ^ (bits // 2)

    first_own = lax.all_gather(jnp.stack(blocks_of(0)), "dp", axis=0, tiled=False)
    later_own = jnp.stack(sum([blocks_of(layer) for layer in range(1, LAYERS)], []) + [prediction_matrix])
    later = lax.all_gather(jnp.stack([later_own, mv.y(later_own)]), "dp", axis=0, tiled=False)
    by_core = first_own.reshape((n_dp // 2, 2) + first_own.shape[1:])
    by_core = lax.dynamic_index_in_dim(by_core, me % 2, 1, keepdims=False)
    crossed = []

    def cross(pair, gate):
        send = by_core[:, 2 * pair : 2 * pair + 2]
        if pair >= 2:
            send = after(send, crossed[pair - 2])
        crossed.append(mv.y(send))
        got = crossed[-1] if gate is None else after(crossed[-1], gate)
        both = (got, mv.core(got))
        own = [[(first_own, 0, (2 * pair + index,))] * n_dp for index in range(2)]
        return [Matrix([own[index], [(array, 1, (index,)) for array in both for _ in range(n_dp // 2)]]) for index in range(2)]

    found = [Matrix([[(later, 0, (half, index))] * n_dp for half in range(2)]) for index in range(later_own.shape[0])]
    layers = [cross] + [found[6 * layer : 6 * layer + 6] for layer in range(LAYERS - 1)]
    head = found[-1]

    counts, pads = filled_sequence_segments[0], leading_filler_number[0]
    ends = jnp.cumsum(counts)
    starts = ends - counts
    first = starts + jnp.minimum(pads, counts - 1)
    cut = jnp.max(jnp.where(ends <= window, ends, 0))
    rows = jnp.where(second, skipped, 0) + jnp.arange(window, dtype=jnp.int32)
    begun = starts[None, :] <= rows[:, None]
    start_row = jnp.max(jnp.where(begun, starts[None, :], 0), axis=1)
    first_row = jnp.max(jnp.where(begun, first[None, :], 0), axis=1)
    real = rows >= first_row
    place = (rows - first_row).astype(F32)
    valid = jnp.where(second, rows >= cut, rows < cut)
    counted = real & valid
    allowed = (start_row[:, None] == start_row[None, :]) & (rows[None, :] <= rows[:, None])
    allowed = allowed & (real[None, :] | (rows[None, :] == rows[:, None]))
    bias = jnp.where(allowed, 0.0, NEG).astype(F32)
    is_first = (first_row[:, None] == rows[None, :]).astype(F32)

    half = HEAD // 2
    width = triple_projector_matrix.shape[3]
    freq = jnp.exp(-jnp.arange(half).astype(F32) * (2.0 * math.log(10000.0) / HEAD))
    angle = place[:, None] * freq[None, :]
    cosine, sine, none = jnp.cos(angle), jnp.sin(angle), jnp.zeros((window, half), F32)
    heads = width // HEAD
    tables = (
        jnp.tile(cosine, (1, 2 * heads)),
        jnp.tile(jnp.concatenate([-sine, none], axis=1), (1, heads)),
        jnp.tile(jnp.concatenate([none, sine], axis=1), (1, heads)),
    )

    points = mine(segment_matrix)
    firsts = jnp.dot(is_first, points, precision=HIGH)
    mean = jnp.mean(firsts, axis=1, keepdims=True)
    centred = firsts - mean
    spread = jnp.sqrt(jnp.mean(centred * centred, axis=1, keepdims=True))
    sigma = jnp.maximum(spread, FLOOR)
    scaled_low = jnp.where(real[:, None], (points - mean) / sigma, 0.0).astype(BF16)

    residual = jnp.einsum("tp,dp->td", scaled_low, embed, preferred_element_type=F32)
    saved = []
    for layer in range(LAYERS):
        residual, kept, layers[layer] = layer_forward(residual, layers[layer], gains[layer], bias, tables, order, width)
        saved.append(kept)

    as_column = lambda flags: flags[:, None].astype(F32)
    wide, flat, column = residual.shape, (window, width), (window, 1)
    rows_of = wide[1] // n_dp
    gain_grads = [[None, None] for _ in range(LAYERS)]
    scatter = Scatter(mv)
    for layer in reversed(range(LAYERS)):
        wq, wk, wv, wo, wu, wd = layers[layer]
        mid, normed_ff, pre, hidden = saved[layer][7:]
        inner = (hidden, pre, normed_ff, mid, gains[layer][1:])
        if layer == LAYERS - 1:
            own, sent, mean_term, sigma_term, grad_res, gain_grads[layer][1], grads = run_kernel(
                head_body,
                (residual, mine(prediction_sensitivity), sens_other, as_column(real), as_column(counted), mean, sigma)
                + inner,
                (head, wd, wu),
                [(flat, F32), (flat, BF16), (column, F32), (column, F32), (wide, F32), ((1, wide[1]), F32)]
                + [((n_dp, 2, 3, rows_of, width), BF16)],
                order,
            )
            proj, grads = attend_backward(grad_res, wo, saved[layer], tables, order, grads)
            early = lax.psum_scatter(grads, "dp", scatter_dimension=0, tiled=True)
            got = mv.y(sent)
            predictions = joined(own, got.astype(F32), cut)
            grad_res = after(grad_res, got)
        else:
            weight = ((2, wide[1] // 2, width), BF16)
            grad_res, gain_grads[layer][1], *grads = run_kernel(
                widen_back_body, (grad_res,) + inner, (wd, wu), [(wide, F32), ((1, wide[1]), F32)] + [weight] * 4, order
            )
            scatter.add(grads[:2], grads[2:])
            proj, *grads = attend_backward(after(grad_res, scatter.cores[-2]), wo, saved[layer], tables, order)
            scatter.add(grads[:2], grads[2:])
            proj = after(proj, scatter.second[-2])
        grad_res, gain_grads[layer][0], *grads = project_backward(
            grad_res, proj, layers[layer], gains[layer], saved[layer], order
        )
        scatter.add(grads[:2], grads[2:])
    grad_low = grad_res.astype(BF16)
    grad_scaled = jnp.einsum("td,dp->tp", grad_low, embed, preferred_element_type=F32)
    embed_term = jnp.einsum("td,tp->dp", grad_low, scaled_low, preferred_element_type=F32)

    grad_scaled = jnp.where(real[:, None], grad_scaled, 0.0)
    mean_row = mean_term - jnp.sum(grad_scaled, axis=1, keepdims=True) / sigma
    sigma_row = sigma_term - jnp.sum(grad_scaled * (points - mean), axis=1, keepdims=True) / (sigma * sigma)
    sums = lax.dot_general(
        is_first, jnp.concatenate([mean_row, sigma_row], axis=1), (((0,), (0,)), ((), ())), precision=HIGH
    )
    pull = jnp.where(spread > FLOOR, (points - mean) / jnp.maximum(spread, FLOOR), 0.0)
    patches = grad_scaled / sigma + sums[:, :1] / patch + sums[:, 1:] * pull / patch
    patches_grad = joined(patches, mv.y(patches), cut)

    tail = jnp.concatenate([embed_term] + [g.T for pair in gain_grads for g in pair], axis=1)
    n = tail.shape[0]
    tail = tail[: n // 2] + mv.core(tail[n // 2 :])
    tail = tail[: n // 4] + mv.x(tail[n // 4 :])
    tail = tail + mv.y(tail)
    n = tail.shape[0] // mv.q
    tail_out = tail[:n]
    for k in range(1, mv.q):
        tail_out = tail_out + mv.z(tail[k * n : (k + 1) * n], mv.q - k)
    w_in_grad = tail_out[:, :patch].T
    gains_grad = tail_out[:, patch:].T.reshape(LAYERS, 2, -1)

    scatter.finish()
    done = scatter.done
    early = early[0, 0].astype(F32) + mv.y(early[0, 1]).astype(F32)
    head_grad, down_last, up_last, attn_last, value_last = early
    qkv, attn = [[done[0][0], done[0][1], value_last]], [attn_last]
    up, down = [up_last], [down_last]
    at = 1
    for layer in reversed(range(LAYERS - 1)):
        down.append(done[at][0])
        up.append(done[at][1])
        attn.append(done[at + 1][0])
        qkv.append([done[at + 2][0], done[at + 2][1], done[at + 1][1]])
        at += 3
    return (
        predictions,
        patches_grad,
        w_in_grad,
        jnp.stack([jnp.stack(parts) for parts in qkv[::-1]]),
        jnp.stack([part.T for part in attn[::-1]]),
        jnp.stack(up[::-1]),
        jnp.stack([part.T for part in down[::-1]]),
        gains_grad,
        head_grad,
    )


def solution(mesh):
    placed = (
        P("dp", None),
        P("dp", None),
        P("dp", None),
        P(None, "dp"),
        P(None, None, "dp", "mp"),
        P(None, "mp", "dp"),
        P(None, "dp", "mp"),
        P(None, "mp", "dp"),
        P(None, None, "dp"),
        P("dp", "mp"),
        P("dp", "mp"),
    )
    return jax.shard_map(
        partial(on_device, n_dp=mesh.shape["dp"]),
        mesh=mesh,
        in_specs=placed,
        out_specs=(
            P("dp", "mp"),
            P("dp", None),
            P(None, "dp"),
            P(None, None, "dp", "mp"),
            P(None, "mp", "dp"),
            P(None, "dp", "mp"),
            P(None, "mp", "dp"),
            P(None, None, "dp"),
            P("dp", "mp"),
        ),
        check_vma=False,
    )
```
